32 devices in a mesh: row: 8 (over y, x, core), col: 4 (over z).
Axes of the slice: x: 2, y: 2, z: 4, core: 2. Of those that a mesh axis runs over, the one named last changes fastest.
Arguments:
- field: bfloat16 [64, 64, 512], P('row', 'col'), may hold values from -6 to 6
- in_weight: bfloat16 [512, 2048], P(None, 'row'), may hold values from -0.25 to 0.25
- conv_weight: float32 [3, 3, 1024], replicated, may hold values from -2 to 2
- proj_weight: bfloat16 [1024, 256], replicated, may hold values from -0.1875 to 0.1875
- dt_weight: bfloat16 [4, 32, 1024], replicated, may hold values from -1 to 1
- dt_bias: float32 [4, 1024], replicated, may hold values from -7 to -2
- decay_rate: float32 [4, 16, 1024], replicated, may hold values from 0.5 to 2
- skip_gain: float32 [4, 1024], replicated, may hold values from 0.1 to 1.9
- norm_gain: float32 [1024], replicated, may hold values from 0.1 to 1.9
- out_weight: bfloat16 [1024, 512], P('col'), may hold values from -0.1875 to 0.1875
- grad_out: bfloat16 [64, 64, 512], P('row', 'col'), may hold values from -6 to 6
Outputs:
- result: bfloat16 [64, 64, 512], P('row', 'col')
- grad_field: float32 [64, 64, 512], P('row', 'col')
- grad_in_weight: float32 [512, 2048], P(None, 'row')
- grad_out_weight: float32 [1024, 512], P('col')
The draws below stay inside these ranges and needn't reach their ends.
All inputs are finite; a program needn't handle non-finite values.
Results may differ from the reference program's by a relative error of at most 0.0073.
Values may be sent and summed in bfloat16 or wider, within the bound.
A program may use at most 256 MiB of HBM per device.

```python
import math
import jax
import jax.numpy as jnp
from jax import lax

C = 512
E = 1024
N = 16
R = 32
K = 4
H = 64
W = 64


def draw_dt_bias(key, part):
    return jax.random.uniform(key, (K, E), jnp.float32, -6.0, -2.0)


def steps_of(own_key, extent, split, least, top_value):
    def one(position, blocks):
        draws = jax.random.uniform(jax.random.fold_in(jax.random.fold_in(own_key, 6), position), (blocks,), jnp.float32, least / len(split), top_value / len(split))
        return jnp.repeat(jnp.exp(draws), extent[position] // blocks).reshape((-1,) + (1,) * (len(extent) - position - 1))

    factor_of = one(*split[0])
    for cut in split[1:]:
        factor_of = factor_of * one(*cut)
    return factor_of


def scatter_about(key, shape, deviation, limit, split=(), dtype=jnp.bfloat16):
    values = jax.random.normal(key, shape, jnp.float32) * deviation
    if len(split) > 0:
        values = steps_of(key, shape, split, -0.22, 0.18) * values
    return jnp.clip(values, min=-limit, max=limit).astype(dtype)


def setup_inputs(seed: int = 0) -> dict:
    key_list = jax.random.split(jax.random.key(seed), 12)
    field = scatter_about(key_list[0], (H, W, C), 1.0, 6.0, ((0, 8), (1, 4)))
    in_weight = scatter_about(key_list[1], (C, 2 * E), C ** -0.5, 0.25, ((1, 8),))
    conv_weight = scatter_about(key_list[2], (3, 3, E), 9 ** -0.5, 2.0, (), jnp.float32)
    proj_weight = scatter_about(key_list[3], (E, K * (R + 2 * N)), E ** -0.5, 0.1875)
    dt_weight = scatter_about(key_list[4], (K, R, E), R ** -0.5, 1.0)
    dt_bias = draw_dt_bias(jax.random.fold_in(key_list[11], 71), 0)
    decay_rate = jnp.clip(jnp.exp(jax.random.uniform(key_list[6], (K, N, E), jnp.float32, math.log(0.5), math.log(2.0))), 0.5, 2.0)
    skip_gain = jnp.clip(1.0 + 0.18 * jax.random.normal(key_list[7], (K, E), jnp.float32), 0.1, 1.9)
    norm_gain = jnp.clip(1.0 + 0.18 * jax.random.normal(key_list[8], (E,), jnp.float32), 0.1, 1.9)
    out_weight = scatter_about(key_list[9], (E, C), E ** -0.5, 0.1875, ((0, 4),))
    grad_out = scatter_about(key_list[10], (H, W, C), 1.0, 6.0, ((0, 8), (1, 4)))
    return {"field": field, "in_weight": in_weight, "conv_weight": conv_weight, "proj_weight": proj_weight, "dt_weight": dt_weight, "dt_bias": dt_bias, "decay_rate": decay_rate, "skip_gain": skip_gain, "norm_gain": norm_gain, "out_weight": out_weight, "grad_out": grad_out}


DT_FLOOR = 0.004
NORM_EPS = 1e-05
TOP_PRECISION = lax.Precision.HIGHEST

def arrange(values, direction):
    if direction >= 2:
        values = jnp.swapaxes(values, 0, 1)
    if direction % 2 == 1:
        values = jnp.flip(values, 0)
    return values

def restore(values, direction):
    if direction % 2 == 1:
        values = jnp.flip(values, 0)
    if direction >= 2:
        values = jnp.swapaxes(values, 0, 1)
    return values

def prepare(projected, dt_matrix, dt_offset):
    rank_part = projected[..., :R]
    step_sizes = DT_FLOOR + jax.nn.softplus(jnp.einsum('plr,re->ple', rank_part, dt_matrix, precision=TOP_PRECISION) + dt_offset)
    return (step_sizes, projected[..., R:R + N], projected[..., R + N:])

def line_sums(inputs, projected, dt_matrix, dt_offset, decay_rates):
    step_sizes, in_coef, _ = prepare(projected, dt_matrix, dt_offset)
    running = jnp.cumsum(step_sizes, axis=0)
    totals = running[-1]
    weights = jnp.exp(-decay_rates * (totals[None, :, None, :] - running[:, :, None, :]))
    driven = (step_sizes * inputs)[:, :, None, :] * in_coef[:, :, :, None]
    return (totals, lax.optimization_barrier(jnp.sum(weights * driven, axis=0)))

def line_outputs(inputs, projected, dt_matrix, dt_offset, decay_rates, skip_row, start_state):
    step_sizes, in_coef, out_coef = prepare(projected, dt_matrix, dt_offset)

    def advance(cell_state, slice_now):
        step_now, input_now, in_now, out_now = slice_now
        cell_state = jnp.exp(-step_now[:, None, :] * decay_rates) * cell_state + (step_now * input_now)[:, None, :] * in_now[:, :, None]
        return (cell_state, jnp.einsum('lne,ln->le', cell_state, out_now, precision=TOP_PRECISION))
    _, outputs = lax.scan(advance, start_state, (step_sizes, inputs, in_coef, out_coef))
    return outputs + skip_row * inputs

def run_lines(inputs, projected, dt_matrix, dt_offset, decay_rates, skip_row):
    line_length = inputs.shape[0]
    line_count = inputs.shape[1]
    block_size = math.gcd(line_count, 8)
    block_count = line_count // block_size

    def solve_block(block_pair):
        part_in, part_proj = block_pair
        totals, end_states = line_sums(part_in, part_proj, dt_matrix, dt_offset, decay_rates)
        start_state = end_states / (1.0 - jnp.exp(-decay_rates * totals[:, None, :]))
        return line_outputs(part_in, part_proj, dt_matrix, dt_offset, decay_rates, skip_row, start_state)
    solve_block = jax.checkpoint(solve_block)
    split_in = inputs.reshape(line_length, block_count, block_size, inputs.shape[2]).transpose(1, 0, 2, 3)
    split_proj = projected.reshape(line_length, block_count, block_size, projected.shape[2]).transpose(1, 0, 2, 3)
    outputs = lax.map(solve_block, (split_in, split_proj))
    return outputs.transpose(1, 0, 2, 3).reshape(line_length, line_count, inputs.shape[2])

def finish(summed, gate_part, norm_gain):
    centre = lax.optimization_barrier(jnp.mean(summed, axis=-1, keepdims=True))
    spread = lax.optimization_barrier(jnp.mean(jnp.square(summed - centre), axis=-1, keepdims=True))
    normed = (summed - centre) * lax.rsqrt(spread + NORM_EPS) * norm_gain
    return normed * jax.nn.silu(gate_part)

def reference(field, in_weight, conv_weight, proj_weight, dt_weight, dt_bias, decay_rate, skip_gain, norm_gain, out_weight, grad_out):
    field_rows = field.reshape(H * W, C)
    mixed_in = jnp.dot(field_rows, in_weight, preferred_element_type=jnp.float32).astype(jnp.bfloat16).reshape(H, W, 2 * E)
    proj_table = proj_weight.astype(jnp.float32)

    def inner_part(source_gate):
        source = source_gate[..., :E]
        gate_part = source_gate[..., E:]
        convolved = jnp.zeros((H, W, E), jnp.float32)
        for row_off in range(3):
            for col_off in range(3):
                convolved = convolved + jnp.roll(source, (1 - row_off, 1 - col_off), axis=(0, 1)) * conv_weight[row_off, col_off]
        active = jax.nn.silu(convolved)
        active = active + lax.stop_gradient(active.astype(jnp.bfloat16).astype(jnp.float32) - active)
        projected = jnp.einsum('hwe,ef->hwf', active, proj_table, precision=TOP_PRECISION).reshape(H, W, K, R + 2 * N)
        summed = jnp.zeros((H, W, E), jnp.float32)
        for direction in range(K):
            lined = run_lines(arrange(active, direction), arrange(projected[:, :, direction, :], direction), dt_weight[direction].astype(jnp.float32), dt_bias[direction], decay_rate[direction], skip_gain[direction])
            summed = summed + restore(lined, direction)
        return finish(summed, gate_part, norm_gain)
    mixed_full, pullback = jax.vjp(inner_part, mixed_in.astype(jnp.float32))
    mixed = mixed_full.astype(jnp.bfloat16).reshape(H * W, E)
    result = (field_rows.astype(jnp.float32) + jnp.dot(mixed, out_weight, preferred_element_type=jnp.float32)).astype(jnp.bfloat16).reshape(H, W, C)
    grad_rows = grad_out.reshape(H * W, C)
    back_mixed = jnp.dot(grad_rows, out_weight.T, preferred_element_type=jnp.float32)
    grad_out_weight = jnp.dot(mixed.T, grad_rows, preferred_element_type=jnp.float32)
    back_xz = pullback(back_mixed.reshape(H, W, E))[0].astype(jnp.bfloat16).reshape(H * W, 2 * E)
    grad_field = (grad_rows.astype(jnp.float32) + jnp.dot(back_xz, in_weight.T, preferred_element_type=jnp.float32)).reshape(H, W, C)
    grad_in_weight = jnp.dot(field_rows.T, back_xz, preferred_element_type=jnp.float32)
    return (result, grad_field, grad_in_weight, grad_out_weight)
```

```python
import math

import jax
import jax.numpy as jnp
from jax import lax
from jax.experimental import pallas as pl
from jax.experimental.pallas import tpu as pltpu
from jax.sharding import PartitionSpec as P

DT_FLOOR = 0.004
NORM_EPS = 1e-05
LOG2E = math.log2(math.e)
LN2 = math.log(2.0)
LANES = 128
F32 = jnp.float32
BF16 = jnp.bfloat16


def softplus(v):
    return jnp.maximum(v, 0.0) + jnp.log1p(jnp.exp(-jnp.abs(v)))


def fill_steps(proj_ref, dtw_ref, bias_ref, raw_ref, step_ref):
    length, lines, width = proj_ref.shape
    chunk = 16

    @pl.loop(0, length // chunk)
    def _(c):
        rows = proj_ref[pl.ds(c * chunk, chunk)].reshape(chunk * lines, width)
        raw = jnp.dot(rows, dtw_ref[...], preferred_element_type=F32) + bias_ref[0:1, :]
        raw = raw.reshape(chunk, lines, raw.shape[-1])
        if raw_ref is not None:
            raw_ref[pl.ds(c * chunk, chunk)] = raw
        step_ref[pl.ds(c * chunk, chunk)] = DT_FLOOR + softplus(raw)


def column(values, i, like):
    return jnp.broadcast_to(values[:, i : i + 1], like.shape)


def forward_kernel(rank, states, act_ref, proj_ref, dtw_ref, bias_ref, rate_ref, skip_ref, y_ref, start_ref, step_ref):
    k = pl.program_id(0)
    length, lines, width = act_ref.shape
    fill_steps(proj_ref, dtw_ref, bias_ref, None, step_ref)
    zero = jnp.zeros((lines, width), F32)

    def place(i):
        return jnp.where(k == 0, i, length - 1 - i)

    def first(i, carry):
        state, total = carry
        p = place(i)
        step = step_ref[p]
        drive = step * act_ref[p].astype(F32)
        coef = proj_ref[p].astype(F32)
        state = tuple(
            jnp.exp2(step * rate_ref[n]) * state[n] + drive * column(coef, rank + n, step)
            for n in range(states)
        )
        return state, total + step

    state, total = lax.fori_loop(0, length, first, ((zero,) * states, zero))
    closed = []
    for n in range(states):
        one = state[n] / (1.0 - jnp.exp2(total * rate_ref[n]))
        start_ref[n] = one
        closed.append(one)

    @pl.when(k == 0)
    def _():
        y_ref[...] = jnp.zeros_like(y_ref)

    skip = jnp.broadcast_to(skip_ref[0:1, :], (lines, width))

    def second(i, state):
        p = place(i)
        step = step_ref[p]
        act = act_ref[p].astype(F32)
        drive = step * act
        coef = proj_ref[p].astype(F32)
        y = y_ref[p] + skip * act
        new = []
        for n in range(states):
            one = jnp.exp2(step * rate_ref[n]) * state[n] + drive * column(coef, rank + n, step)
            y = y + one * column(coef, rank + states + n, step)
            new.append(one)
        y_ref[p] = y
        return tuple(new)

    lax.fori_loop(0, length, second, tuple(closed))


def backward_kernel(
    rank, states, act_ref, proj_ref, dtw_ref, dtwt_ref, bias_ref, rate_ref, skip_ref, start_ref, gy_ref, pick_ref,
    dact_ref, dproj_ref, raw_ref, step_ref, h_ref, a_ref, prod_ref, draw_ref,
):
    k = pl.program_id(0)
    length, lines, width = act_ref.shape
    fill_steps(proj_ref, dtw_ref, bias_ref, raw_ref, step_ref)
    zero = jnp.zeros((lines, width), F32)

    def place(i):
        return jnp.where(k == 0, i, length - 1 - i)

    for n in range(states):
        h_ref[0, n] = start_ref[n]

    def replay(i, carry):
        state, total = carry
        p = place(i)
        step = step_ref[p]
        drive = step * act_ref[p].astype(F32)
        coef = proj_ref[p].astype(F32)
        new = []
        for n in range(states):
            decay = jnp.exp2(step * rate_ref[n])
            one = decay * state[n] + drive * column(coef, rank + n, step)
            a_ref[i, n] = decay
            h_ref[i + 1, n] = one
            new.append(one)
        return tuple(new), total + step

    _, total = lax.fori_loop(0, length, replay, (tuple(start_ref[n] for n in range(states)), zero))

    def adjoint(j, back):
        i = length - 1 - j
        p = place(i)
        gy = gy_ref[p].astype(F32)
        coef = proj_ref[p].astype(F32)
        return tuple(
            a_ref[i, n] * (back[n] + gy * column(coef, rank + states + n, gy)) for n in range(states)
        )

    back = lax.fori_loop(0, length, adjoint, (zero,) * states)
    back = tuple(back[n] / (1.0 - jnp.exp2(total * rate_ref[n])) for n in range(states))

    @pl.when(k == 0)
    def _():
        dact_ref[...] = jnp.zeros_like(dact_ref)

    skip = jnp.broadcast_to(skip_ref[0:1, :], (lines, width))

    def last(j, back):
        i = length - 1 - j
        p = place(i)
        gy = gy_ref[p].astype(F32)
        coef = proj_ref[p].astype(F32)
        step = step_ref[p]
        act = act_ref[p].astype(F32)
        drive = step * act
        ddrive = zero
        dstep = zero
        new = []
        for n in range(states):
            lam = back[n] + gy * column(coef, rank + states + n, gy)
            prod_ref[p, :, pl.ds(n * width, width)] = (drive * lam).astype(BF16)
            prod_ref[p, :, pl.ds((states + n) * width, width)] = (gy * h_ref[i + 1, n]).astype(BF16)
            ddrive = ddrive + lam * column(coef, rank + n, gy)
            carried = a_ref[i, n] * lam
            dstep = dstep + (carried * h_ref[i, n]) * rate_ref[n]
            new.append(carried)
        dstep = LN2 * dstep + act * ddrive
        dact_ref[p] = dact_ref[p] + step * ddrive + skip * gy
        draw_ref[p] = (dstep / (1.0 + jnp.exp(-raw_ref[p]))).astype(BF16)
        return tuple(new)

    lax.fori_loop(0, length, last, back)
    chunk = 8

    @pl.loop(0, length // chunk)
    def _(c):
        at = pl.ds(c * chunk, chunk)
        prods = prod_ref[at].reshape(chunk * lines, prod_ref.shape[-1])
        raws = draw_ref[at].reshape(chunk * lines, width)
        out = jnp.dot(prods, pick_ref[...], preferred_element_type=F32)
        out = out + jnp.dot(raws, dtwt_ref[...], preferred_element_type=F32)
        dproj_ref[at] = out.reshape(chunk, lines, out.shape[-1])


def whole_spec(shape):
    return pl.BlockSpec(shape, lambda k: (0,) * len(shape))


def each_spec(shape):
    return pl.BlockSpec((None,) + shape, lambda k: (k,) + (0,) * len(shape))


def run_forward(act, proj, params):
    dtw, dtwt, bias, rates, skip, rank, states = params
    length, lines, width = act.shape
    coefs = proj.shape[-1]
    work = 2 * 2 * length * lines * width * states
    return pl.pallas_call(
        lambda *refs: forward_kernel(rank, states, *refs),
        grid=(2,),
        in_specs=[
            whole_spec(act.shape),
            each_spec((length, lines, coefs)),
            each_spec((coefs, width)),
            each_spec((8, width)),
            each_spec((states, lines, width)),
            each_spec((8, width)),
        ],
        out_specs=[whole_spec(act.shape), each_spec((states, lines, width))],
        out_shape=[
            jax.ShapeDtypeStruct(act.shape, F32),
            jax.ShapeDtypeStruct((2, states, lines, width), F32),
        ],
        scratch_shapes=[pltpu.VMEM(act.shape, F32)],
        compiler_params=pltpu.CompilerParams(vmem_limit_bytes=40 * 2**20),
        cost_estimate=pl.CostEstimate(flops=10 * work, bytes_accessed=4 * act.size * 4, transcendentals=work),
        name="scan_forward",
    )(act, proj, dtw, bias, rates, skip)


def run_backward(act, proj, params, start, gy, pick):
    dtw, dtwt, bias, rates, skip, rank, states = params
    length, lines, width = act.shape
    coefs = proj.shape[-1]
    work = 2 * 3 * length * lines * width * states
    return pl.pallas_call(
        lambda *refs: backward_kernel(rank, states, *refs),
        grid=(2,),
        in_specs=[
            whole_spec(act.shape),
            each_spec((length, lines, coefs)),
            each_spec((coefs, width)),
            each_spec((width, coefs)),
            each_spec((8, width)),
            each_spec((states, lines, width)),
            each_spec((8, width)),
            each_spec((states, lines, width)),
            whole_spec(act.shape),
            whole_spec(pick.shape),
        ],
        out_specs=[whole_spec(act.shape), each_spec((length, lines, coefs))],
        out_shape=[
            jax.ShapeDtypeStruct(act.shape, F32),
            jax.ShapeDtypeStruct((2, length, lines, coefs), F32),
        ],
        scratch_shapes=[
            pltpu.VMEM(act.shape, F32),
            pltpu.VMEM(act.shape, F32),
            pltpu.VMEM((length + 1, states, lines, width), F32),
            pltpu.VMEM((length, states, lines, width), F32),
            pltpu.VMEM((length, lines, 2 * states * width), BF16),
            pltpu.VMEM(act.shape, BF16),
        ],
        compiler_params=pltpu.CompilerParams(vmem_limit_bytes=60 * 2**20),
        cost_estimate=pl.CostEstimate(flops=10 * work, bytes_accessed=8 * act.size * 4, transcendentals=work),
        name="scan_backward",
    )(act, proj, dtw, dtwt, bias, rates, skip, start, gy, pick)


def pad_to(values, axis, size, fill=0.0):
    missing = size - values.shape[axis]
    if missing == 0:
        return values
    pads = [(0, 0)] * values.ndim
    pads[axis] = (0, missing)
    return jnp.pad(values, pads, constant_values=fill)


def swap(values):
    return jnp.swapaxes(values, 0, 1)


def weight_moves(peers):
    half = peers // 2
    one = [(r, 2 * r if r < half else 2 * (r - half) + 1) for r in range(peers)]
    two = [(r, 2 * r + 1 if r < half else 2 * (r - half)) for r in range(peers)]
    return one, two


def reverse_moves(moves):
    return [(b, a) for a, b in moves]


def col_halo(cells):
    peers = lax.axis_size("col")
    up = [(i, (i + 1) % peers) for i in range(peers)]
    down = [((i + 1) % peers, i) for i in range(peers)]
    before = lax.ppermute(cells[:, -1:], "col", up)
    after = lax.ppermute(cells[:, :1], "col", down)
    wide = jnp.concatenate([before, cells, after], axis=1)
    return jnp.concatenate([wide[-1:], wide, wide[:1]], axis=0)


def local(
    field, in_weight, conv_weight, proj_weight, dt_weight, dt_bias, decay_rate, skip_gain, norm_gain, out_weight, grad_out,
):
    rows, cols, c_dim = field.shape
    dirs, rank, e_dim = dt_weight.shape
    states = decay_rate.shape[1]
    coefs = rank + 2 * states
    nr, nc = lax.axis_size("row"), lax.axis_size("col")
    me = lax.axis_index("row")
    all_rows, width = rows * nr, e_dim // nr
    even = me % 2 == 0
    low = me < nr // 2
    moves_one, moves_two = weight_moves(nr)

    def mine(values):
        return lax.dynamic_slice_in_dim(values, me * width, width, axis=values.ndim - 1)

    field_all = lax.all_gather(field, "row", axis=0, tiled=True)
    left, right = in_weight[:, :width], in_weight[:, width:]
    got_one = lax.ppermute(jnp.where(low, left, right), "row", moves_one)
    got_two = lax.ppermute(jnp.where(low, right, left), "row", moves_two)
    w_mine = jnp.concatenate(
        [jnp.where(even, got_one, got_two), jnp.where(even, got_two, got_one)], axis=1
    )
    field_flat = field_all.reshape(-1, c_dim)
    xz = jnp.dot(field_flat, w_mine, preferred_element_type=F32).astype(BF16).reshape(all_rows, cols, 2 * width)
    source, gate = xz[..., :width], xz[..., width:].astype(F32)
    grad_all = lax.all_gather(grad_out, "row", axis=0, tiled=True)
    out_full = lax.all_gather(out_weight, "col", axis=0, tiled=True)
    w_perm = lax.all_gather(w_mine, "row", axis=1, tiled=True)

    taps = mine(conv_weight)
    padded = col_halo(source)
    convolved = jnp.zeros(source.shape, F32)
    for a in range(3):
        for b in range(3):
            convolved = convolved + padded[a : a + all_rows, b : b + cols].astype(F32) * taps[a, b]
    active = jax.nn.silu(convolved).astype(BF16)

    act_cells = lax.all_to_all(active, "row", 0, 2, tiled=True)
    proj_cells = jnp.dot(act_cells.reshape(-1, e_dim), proj_weight, preferred_element_type=F32)
    proj = lax.all_gather(
        proj_cells.astype(BF16).reshape(rows, cols, dirs * coefs), "row", axis=0, tiled=True
    )
    split = 2 * coefs
    across = lax.all_to_all(
        jnp.concatenate([active, proj[..., split:]], axis=-1), "col", 0, 1, tiled=True
    )
    across = swap(across)
    act_down, act_across = active, across[..., :width]
    pair = lambda values: jnp.stack([values[..., :coefs], values[..., coefs:]], axis=0)
    proj_down, proj_across = pair(proj[..., :split]), pair(across[..., width:])

    lanes = -(-width // LANES) * LANES
    lines = cols
    dtw = pad_to(pad_to(mine(dt_weight), 2, lanes), 1, coefs)
    dtwt = jnp.swapaxes(dtw, 1, 2)
    bias = jnp.broadcast_to(pad_to(mine(dt_bias), 1, lanes)[:, None, :], (dirs, 8, lanes))
    rates = -LOG2E * pad_to(mine(decay_rate), 2, lanes, 1.0)
    skip = jnp.broadcast_to(pad_to(mine(skip_gain), 1, lanes)[:, None, :], (dirs, 8, lanes))

    def params(at, count):
        wide = jnp.broadcast_to(rates[at : at + 2][:, :, None, :], (2, states, count, lanes))
        cut = slice(at, at + 2)
        return dtw[cut], dtwt[cut], bias[cut], wide, skip[cut], rank, states

    params_down, params_across = params(0, act_down.shape[1]), params(2, act_across.shape[1])
    act_down, act_across = pad_to(act_down, 2, lanes), pad_to(act_across, 2, lanes)
    y_down, start_down = run_forward(act_down, proj_down, params_down)
    y_across, start_across = run_forward(act_across, proj_across, params_across)
    y_back = lax.all_to_all(swap(y_across[..., :width].astype(BF16)), "col", 1, 0, tiled=True)
    summed = y_down[..., :width] + y_back.astype(F32)

    back_mixed = lax.dot_general(
        grad_all.reshape(-1, c_dim),
        lax.dynamic_slice_in_dim(out_full, me * width, width, axis=0),
        (((1,), (1,)), ((), ())),
        preferred_element_type=F32,
    ).reshape(all_rows, cols, width)
    gain = mine(norm_gain)
    sig = jax.nn.sigmoid(gate)
    silu = gate * sig
    back_norm = back_mixed * silu * gain
    own_mean = jnp.mean(summed, axis=-1)
    shifted = summed - own_mean[..., None]
    stats = jnp.stack(
        [own_mean, jnp.sum(shifted * shifted, -1), jnp.sum(back_norm, -1), jnp.sum(back_norm * shifted, -1)]
    )
    stats = lax.all_gather(stats, "row", axis=0)
    means = stats[:, 0]
    centre = jnp.mean(means, axis=0)
    off = means - centre
    variance = (jnp.sum(stats[:, 1], 0) + width * jnp.sum(off * off, 0)) / e_dim
    scale = lax.rsqrt(variance + NORM_EPS)
    flat_mean = jnp.sum(stats[:, 2], 0) / e_dim
    tilt_mean = scale * jnp.sum(stats[:, 3] + off * stats[:, 2], 0) / e_dim
    hat = (summed - centre[..., None]) * scale[..., None]
    normed = hat * gain
    mixed = (normed * silu).astype(BF16)
    back_gate = back_mixed * normed * (sig * (1.0 + gate * (1.0 - sig)))
    back_summed = scale[..., None] * (back_norm - flat_mean[..., None] - hat * tilt_mean[..., None])
    back_bf = back_summed.astype(BF16)
    gy_across = swap(lax.all_to_all(back_bf, "col", 0, 1, tiled=True))

    spots = jnp.repeat(jnp.arange(2 * states) + rank, lanes)
    pick = (spots[:, None] == jnp.arange(coefs)[None, :]).astype(BF16)
    dact_across, dproj_across = run_backward(
        act_across, proj_across, params_across, start_across, pad_to(gy_across, 2, lanes), pick
    )
    dact_down, dproj_down = run_backward(
        act_down, proj_down, params_down, start_down, pad_to(back_bf, 2, lanes), pick
    )
    unpair = lambda values: jnp.concatenate([values[0], values[1]], axis=-1)
    returned = lax.all_to_all(
        swap(jnp.concatenate([dact_across[..., :width], unpair(dproj_across)], axis=-1).astype(BF16)),
        "col", 1, 0, tiled=True,
    )
    dproj = jnp.concatenate([unpair(dproj_down), returned[..., width:].astype(F32)], axis=-1)
    dproj = lax.psum_scatter(dproj, "row", scatter_dimension=0, tiled=True)
    dproj = lax.all_gather(dproj.astype(BF16), "row", axis=0, tiled=True)
    proj_rows = lax.dynamic_slice_in_dim(proj_weight, me * width, width, axis=0)
    back_active = lax.dot_general(
        dproj.reshape(-1, dirs * coefs), proj_rows, (((1,), (1,)), ((), ())), preferred_element_type=F32
    ).reshape(all_rows, cols, width)
    back_active = back_active + dact_down[..., :width] + returned[..., :width].astype(F32)
    conv_sig = jax.nn.sigmoid(convolved)
    back_conv = back_active * (conv_sig * (1.0 + convolved * (1.0 - conv_sig)))
    grad_padded = col_halo(back_conv)
    back_source = jnp.zeros(source.shape, F32)
    for a in range(3):
        for b in range(3):
            back_source = back_source + grad_padded[2 - a : 2 - a + all_rows, 2 - b : 2 - b + cols] * taps[a, b]
    back_xz = jnp.concatenate([back_source.astype(BF16), back_gate.astype(BF16)], axis=-1)

    mixed_cells = lax.all_to_all(mixed, "row", 0, 2, tiled=True).reshape(-1, e_dim)
    result = field.astype(F32) + jnp.dot(mixed_cells, out_full, preferred_element_type=F32).reshape(field.shape)
    xz_cells = lax.all_to_all(back_xz, "row", 0, 2, tiled=True).reshape(-1, 2 * e_dim)
    grad_field = grad_out.astype(F32) + lax.dot_general(
        xz_cells, w_perm, (((1,), (1,)), ((), ())), preferred_element_type=F32
    ).reshape(field.shape)
    contract = (((0,), (0,)), ((), ()))
    in_part = lax.dot_general(
        field_flat, back_xz.reshape(-1, 2 * width), contract, preferred_element_type=F32
    )
    in_sum = lax.psum(in_part, "col")
    g_src, g_gate = in_sum[:, :width], in_sum[:, width:]
    back_one = lax.ppermute(jnp.where(even, g_src, g_gate), "row", reverse_moves(moves_one))
    back_two = lax.ppermute(jnp.where(even, g_gate, g_src), "row", reverse_moves(moves_two))
    grad_in = jnp.concatenate(
        [jnp.where(low, back_one, back_two), jnp.where(low, back_two, back_one)], axis=1
    )
    out_part = lax.dot_general(
        mixed.reshape(-1, width), grad_all.reshape(-1, c_dim), contract, preferred_element_type=F32
    )
    out_sum = lax.psum_scatter(out_part, "col", scatter_dimension=0, tiled=True)
    out_rows = lax.all_gather(out_sum, "row", axis=0)
    grad_out_w = lax.all_to_all(out_rows, "col", 0, 1, tiled=True).reshape(e_dim // nc, c_dim)
    return (result.astype(BF16), grad_field, grad_in, grad_out_w)


def solution(mesh):
    in_specs = (
        P("row", "col", None), P(None, "row"), P(), P(), P(), P(), P(), P(), P(), P("col", None), P("row", "col", None),
    )
    out_specs = (P("row", "col", None), P("row", "col", None), P(None, "row"), P("col", None))
    return jax.shard_map(local, mesh=mesh, in_specs=in_specs, out_specs=out_specs, check_vma=False)
```

```python
import math

import jax
import jax.numpy as jnp
from jax import lax
from jax.experimental import pallas as pl
from jax.experimental.pallas import tpu as pltpu
from jax.sharding import PartitionSpec as P

DT_FLOOR = 0.004
NORM_EPS = 1e-05
LOG2E = math.log2(math.e)
LN2 = math.log(2.0)
LANES = 128
F32 = jnp.float32
BF16 = jnp.bfloat16


def softplus(v):
    return jnp.maximum(v, 0.0) + jnp.log1p(jnp.exp(-jnp.abs(v)))


def fill_steps(proj_ref, dtw_ref, bias_ref, raw_ref, step_ref):
    length, lines, width = proj_ref.shape
    chunk = 16

    @pl.loop(0, length // chunk)
    def _(c):
        rows = proj_ref[pl.ds(c * chunk, chunk)].reshape(chunk * lines, width)
        raw = jnp.dot(rows, dtw_ref[...], preferred_element_type=F32) + bias_ref[0:1, :]
        raw = raw.reshape(chunk, lines, raw.shape[-1])
        if raw_ref is not None:
            raw_ref[pl.ds(c * chunk, chunk)] = raw
        step_ref[pl.ds(c * chunk, chunk)] = DT_FLOOR + softplus(raw)


def spread_coefs(proj_ref, spread_ref, wide_ref):
    length, lines, coefs = proj_ref.shape
    chunk = 16

    @pl.loop(0, length // chunk)
    def _(c):
        at = pl.ds(c * chunk, chunk)
        rows = proj_ref[at].reshape(chunk * lines, coefs)
        for n in range(wide_ref.shape[-1] // 512):
            cut = pl.ds(n * 512, 512)
            out = jnp.dot(rows, spread_ref[:, cut], preferred_element_type=F32)
            wide_ref[at, :, cut] = out.reshape(chunk, lines, 512)


def loop(count, body, carry, unroll):
    def several(i, carry):
        for j in range(unroll):
            carry = body(i * unroll + j, carry)
        return carry

    return lax.fori_loop(0, count // unroll, several, carry)


def forward_kernel(
    states, act_ref, proj_ref, dtw_ref, bias_ref, rate_ref, skip_ref, spread_ref, y_ref, start_ref, step_ref, wide_ref,
):
    k = pl.program_id(0)
    length, lines, width = act_ref.shape
    fill_steps(proj_ref, dtw_ref, bias_ref, None, step_ref)
    spread_coefs(proj_ref, spread_ref, wide_ref)
    zero = jnp.zeros((lines, width), F32)

    def place(i):
        return jnp.where(k == 0, i, length - 1 - i)

    def coef(p, n):
        return wide_ref[p, :, pl.ds(n * width, width)]

    def first(i, carry):
        state, total = carry
        p = place(i)
        step = step_ref[p]
        drive = step * act_ref[p].astype(F32)
        state = tuple(
            jnp.exp2(step * rate_ref[n]) * state[n] + drive * coef(p, n) for n in range(states)
        )
        return state, total + step

    state, total = loop(length, first, ((zero,) * states, zero), 2)
    closed = []
    for n in range(states):
        one = state[n] / (1.0 - jnp.exp2(total * rate_ref[n]))
        start_ref[n] = one
        closed.append(one)

    @pl.when(k == 0)
    def _():
        y_ref[...] = jnp.zeros_like(y_ref)

    skip = jnp.broadcast_to(skip_ref[0:1, :], (lines, width))

    def second(i, state):
        p = place(i)
        step = step_ref[p]
        act = act_ref[p].astype(F32)
        drive = step * act
        y = y_ref[p] + skip * act
        new = []
        for n in range(states):
            one = jnp.exp2(step * rate_ref[n]) * state[n] + drive * coef(p, n)
            y = y + one * coef(p, states + n)
            new.append(one)
        y_ref[p] = y
        return tuple(new)

    loop(length, second, tuple(closed), 2)


def backward_kernel(
    states, act_ref, proj_ref, dtw_ref, dtwt_ref, bias_ref, rate_ref, skip_ref, start_ref, gy_ref, pick_ref, spread_ref,
    dact_ref, dproj_ref, raw_ref, step_ref, h_ref, wide_ref, prod_ref, draw_ref,
):
    k = pl.program_id(0)
    length, lines, width = act_ref.shape
    fill_steps(proj_ref, dtw_ref, bias_ref, raw_ref, step_ref)
    spread_coefs(proj_ref, spread_ref, wide_ref)
    zero = jnp.zeros((lines, width), F32)

    def place(i):
        return jnp.where(k == 0, i, length - 1 - i)

    def coef(p, n):
        return wide_ref[p, :, pl.ds(n * width, width)]

    for n in range(states):
        h_ref[0, n] = start_ref[n].astype(BF16)

    def replay(i, carry):
        state, total = carry
        p = place(i)
        step = step_ref[p]
        drive = step * act_ref[p].astype(F32)
        new = []
        for n in range(states):
            one = jnp.exp2(step * rate_ref[n]) * state[n] + drive * coef(p, n)
            h_ref[i + 1, n] = one.astype(BF16)
            new.append(one)
        return tuple(new), total + step

    _, total = loop(length, replay, (tuple(start_ref[n] for n in range(states)), zero), 2)

    def adjoint(j, back):
        p = place(length - 1 - j)
        gy = gy_ref[p].astype(F32)
        step = step_ref[p]
        return tuple(
            jnp.exp2(step * rate_ref[n]) * (back[n] + gy * coef(p, states + n)) for n in range(states)
        )

    back = loop(length, adjoint, (zero,) * states, 2)
    back = tuple(back[n] / (1.0 - jnp.exp2(total * rate_ref[n])) for n in range(states))

    @pl.when(k == 0)
    def _():
        dact_ref[...] = jnp.zeros_like(dact_ref)

    skip = jnp.broadcast_to(skip_ref[0:1, :], (lines, width))
    chunk = prod_ref.shape[0]

    def part(c, back):
        first_j = c * chunk

        def last(q, back):
            i = length - 1 - (first_j + q)
            p = place(i)
            gy = gy_ref[p].astype(F32)
            step = step_ref[p]
            act = act_ref[p].astype(F32)
            drive = step * act
            ddrive = zero
            dstep = zero
            new = []
            for n in range(states):
                rate = rate_ref[n]
                lam = back[n] + gy * coef(p, states + n)
                prod_ref[q, :, pl.ds(n * width, width)] = (drive * lam).astype(BF16)
                prod_ref[q, :, pl.ds((states + n) * width, width)] = (gy * h_ref[i + 1, n].astype(F32)).astype(BF16)
                ddrive = ddrive + lam * coef(p, n)
                carried = jnp.exp2(step * rate) * lam
                dstep = dstep + (carried * h_ref[i, n].astype(F32)) * rate
                new.append(carried)
            dstep = LN2 * dstep + act * ddrive
            dact_ref[p] = dact_ref[p] + step * ddrive + skip * gy
            draw_ref[q] = (dstep / (1.0 + jnp.exp(-raw_ref[p]))).astype(BF16)
            return tuple(new)

        back = loop(chunk, last, back, 2)
        prods = prod_ref[...].reshape(chunk * lines, prod_ref.shape[-1])
        raws = draw_ref[...].reshape(chunk * lines, width)
        out = jnp.dot(prods, pick_ref[...], preferred_element_type=F32)
        out = out + jnp.dot(raws, dtwt_ref[...], preferred_element_type=F32)
        out = out.reshape(chunk, lines, out.shape[-1])
        for q in range(chunk):
            dproj_ref[place(length - 1 - (first_j + q))] = out[q]
        return back

    lax.fori_loop(0, length // chunk, part, back)


def whole_spec(shape):
    return pl.BlockSpec(shape, lambda k: (0,) * len(shape))


def each_spec(shape):
    return pl.BlockSpec((None,) + shape, lambda k: (k,) + (0,) * len(shape))


def run_forward(act, proj, params, spread):
    dtw, dtwt, bias, rates, skip, rank, states = params
    length, lines, width = act.shape
    coefs = proj.shape[-1]
    work = 2 * 2 * length * lines * width * states
    return pl.pallas_call(
        lambda *refs: forward_kernel(states, *refs),
        grid=(2,),
        in_specs=[
            whole_spec(act.shape),
            each_spec((length, lines, coefs)),
            each_spec((coefs, width)),
            each_spec((8, width)),
            each_spec((states, lines, width)),
            each_spec((8, width)),
            whole_spec(spread.shape),
        ],
        out_specs=[whole_spec(act.shape), each_spec((states, lines, width))],
        out_shape=[
            jax.ShapeDtypeStruct(act.shape, F32),
            jax.ShapeDtypeStruct((2, states, lines, width), F32),
        ],
        scratch_shapes=[
            pltpu.VMEM(act.shape, F32),
            pltpu.VMEM((length, lines, 2 * states * width), F32),
        ],
        compiler_params=pltpu.CompilerParams(vmem_limit_bytes=56 * 2**20),
        cost_estimate=pl.CostEstimate(flops=10 * work, bytes_accessed=4 * act.size * 4, transcendentals=work),
        name="scan_forward",
    )(act, proj, dtw, bias, rates, skip, spread)


def run_backward(act, proj, params, start, gy, pick, spread):
    dtw, dtwt, bias, rates, skip, rank, states = params
    length, lines, width = act.shape
    coefs = proj.shape[-1]
    work = 2 * 3 * length * lines * width * states
    return pl.pallas_call(
        lambda *refs: backward_kernel(states, *refs),
        grid=(2,),
        in_specs=[
            whole_spec(act.shape),
            each_spec((length, lines, coefs)),
            each_spec((coefs, width)),
            each_spec((width, coefs)),
            each_spec((8, width)),
            each_spec((states, lines, width)),
            each_spec((8, width)),
            each_spec((states, lines, width)),
            whole_spec(act.shape),
            whole_spec(pick.shape),
            whole_spec(spread.shape),
        ],
        out_specs=[whole_spec(act.shape), each_spec((length, lines, coefs))],
        out_shape=[
            jax.ShapeDtypeStruct(act.shape, F32),
            jax.ShapeDtypeStruct((2, length, lines, coefs), F32),
        ],
        scratch_shapes=[
            pltpu.VMEM(act.shape, F32),
            pltpu.VMEM(act.shape, F32),
            pltpu.VMEM((length + 1, states, lines, width), BF16),
            pltpu.VMEM((length, lines, 2 * states * width), F32),
            pltpu.VMEM((8, lines, 2 * states * width), BF16),
            pltpu.VMEM((8, lines, width), BF16),
        ],
        compiler_params=pltpu.CompilerParams(vmem_limit_bytes=60 * 2**20),
        cost_estimate=pl.CostEstimate(flops=10 * work, bytes_accessed=8 * act.size * 4, transcendentals=work),
        name="scan_backward",
    )(act, proj, dtw, dtwt, bias, rates, skip, start, gy, pick, spread)


def pad_to(values, axis, size, fill=0.0):
    missing = size - values.shape[axis]
    if missing == 0:
        return values
    pads = [(0, 0)] * values.ndim
    pads[axis] = (0, missing)
    return jnp.pad(values, pads, constant_values=fill)


def swap(values):
    return jnp.swapaxes(values, 0, 1)


def weight_moves(peers):
    half = peers // 2
    one = [(r, 2 * r if r < half else 2 * (r - half) + 1) for r in range(peers)]
    two = [(r, 2 * r + 1 if r < half else 2 * (r - half)) for r in range(peers)]
    return one, two


def reverse_moves(moves):
    return [(b, a) for a, b in moves]


def col_halo(cells):
    peers = lax.axis_size("col")
    up = [(i, (i + 1) % peers) for i in range(peers)]
    down = [((i + 1) % peers, i) for i in range(peers)]
    before = lax.ppermute(cells[:, -1:], "col", up)
    after = lax.ppermute(cells[:, :1], "col", down)
    wide = jnp.concatenate([before, cells, after], axis=1)
    return jnp.concatenate([wide[-1:], wide, wide[:1]], axis=0)


def local(
    field, in_weight, conv_weight, proj_weight, dt_weight, dt_bias, decay_rate, skip_gain, norm_gain, out_weight, grad_out,
):
    rows, cols, c_dim = field.shape
    dirs, rank, e_dim = dt_weight.shape
    states = decay_rate.shape[1]
    coefs = rank + 2 * states
    nr, nc = lax.axis_size("row"), lax.axis_size("col")
    me = lax.axis_index("row")
    all_rows, width = rows * nr, e_dim // nr
    even = me % 2 == 0
    low = me < nr // 2
    moves_one, moves_two = weight_moves(nr)

    def mine(values):
        return lax.dynamic_slice_in_dim(values, me * width, width, axis=values.ndim - 1)

    field_all = lax.all_gather(field, "row", axis=0, tiled=True)
    left, right = in_weight[:, :width], in_weight[:, width:]
    got_one = lax.ppermute(jnp.where(low, left, right), "row", moves_one)
    got_two = lax.ppermute(jnp.where(low, right, left), "row", moves_two)
    w_mine = jnp.concatenate(
        [jnp.where(even, got_one, got_two), jnp.where(even, got_two, got_one)], axis=1
    )
    field_flat = field_all.reshape(-1, c_dim)
    xz = jnp.dot(field_flat, w_mine, preferred_element_type=F32).astype(BF16).reshape(all_rows, cols, 2 * width)
    source, gate = xz[..., :width], xz[..., width:].astype(F32)
    grad_all = lax.all_gather(grad_out, "row", axis=0, tiled=True)
    out_full = lax.all_gather(out_weight, "col", axis=0, tiled=True)
    w_perm = lax.all_gather(w_mine, "row", axis=1, tiled=True)

    taps = mine(conv_weight)
    padded = col_halo(source)
    convolved = jnp.zeros(source.shape, F32)
    for a in range(3):
        for b in range(3):
            convolved = convolved + padded[a : a + all_rows, b : b + cols].astype(F32) * taps[a, b]
    active = jax.nn.silu(convolved).astype(BF16)

    act_cells = lax.all_to_all(active, "row", 0, 2, tiled=True)
    proj_cells = jnp.dot(act_cells.reshape(-1, e_dim), proj_weight, preferred_element_type=F32)
    proj = lax.all_gather(
        proj_cells.astype(BF16).reshape(rows, cols, dirs * coefs), "row", axis=0, tiled=True
    )
    split = 2 * coefs
    across = lax.all_to_all(
        jnp.concatenate([active, proj[..., split:]], axis=-1), "col", 0, 1, tiled=True
    )
    across = swap(across)
    act_down, act_across = active, across[..., :width]
    pair = lambda values: jnp.stack([values[..., :coefs], values[..., coefs:]], axis=0)
    proj_down, proj_across = pair(proj[..., :split]), pair(across[..., width:])

    lanes = -(-width // LANES) * LANES
    lines = cols
    dtw = pad_to(pad_to(mine(dt_weight), 2, lanes), 1, coefs)
    dtwt = jnp.swapaxes(dtw, 1, 2)
    bias = jnp.broadcast_to(pad_to(mine(dt_bias), 1, lanes)[:, None, :], (dirs, 8, lanes))
    rates = -LOG2E * pad_to(mine(decay_rate), 2, lanes, 1.0)
    skip = jnp.broadcast_to(pad_to(mine(skip_gain), 1, lanes)[:, None, :], (dirs, 8, lanes))

    def params(at, count):
        wide = jnp.broadcast_to(rates[at : at + 2][:, :, None, :], (2, states, count, lanes))
        cut = slice(at, at + 2)
        return dtw[cut], dtwt[cut], bias[cut], wide, skip[cut], rank, states

    params_down, params_across = params(0, act_down.shape[1]), params(2, act_across.shape[1])
    act_down, act_across = pad_to(act_down, 2, lanes), pad_to(act_across, 2, lanes)
    spots = jnp.repeat(jnp.arange(2 * states) + rank, lanes)
    pick = (spots[:, None] == jnp.arange(coefs)[None, :]).astype(BF16)
    spread = pick.T
    y_across, start_across = run_forward(act_across, proj_across, params_across, spread)
    y_down, start_down = run_forward(act_down, proj_down, params_down, spread)
    y_back = lax.all_to_all(swap(y_across[..., :width].astype(BF16)), "col", 1, 0, tiled=True)
    summed = y_down[..., :width] + y_back.astype(F32)

    back_mixed = lax.dot_general(
        grad_all.reshape(-1, c_dim),
        lax.dynamic_slice_in_dim(out_full, me * width, width, axis=0),
        (((1,), (1,)), ((), ())),
        preferred_element_type=F32,
    ).reshape(all_rows, cols, width)
    gain = mine(norm_gain)
    sig = jax.nn.sigmoid(gate)
    silu = gate * sig
    back_norm = back_mixed * silu * gain
    own_mean = jnp.mean(summed, axis=-1)
    shifted = summed - own_mean[..., None]
    stats = jnp.stack(
        [own_mean, jnp.sum(shifted * shifted, -1), jnp.sum(back_norm, -1), jnp.sum(back_norm * shifted, -1)]
    )
    stats = lax.all_gather(stats, "row", axis=0)
    means = stats[:, 0]
    centre = jnp.mean(means, axis=0)
    off = means - centre
    variance = (jnp.sum(stats[:, 1], 0) + width * jnp.sum(off * off, 0)) / e_dim
    scale = lax.rsqrt(variance + NORM_EPS)
    flat_mean = jnp.sum(stats[:, 2], 0) / e_dim
    tilt_mean = scale * jnp.sum(stats[:, 3] + off * stats[:, 2], 0) / e_dim
    hat = (summed - centre[..., None]) * scale[..., None]
    normed = hat * gain
    mixed = (normed * silu).astype(BF16)
    back_gate = back_mixed * normed * (sig * (1.0 + gate * (1.0 - sig)))
    back_summed = scale[..., None] * (back_norm - flat_mean[..., None] - hat * tilt_mean[..., None])
    back_bf = back_summed.astype(BF16)
    gy_across = swap(lax.all_to_all(back_bf, "col", 0, 1, tiled=True))

    dact_across, dproj_across = run_backward(
        act_across, proj_across, params_across, start_across, pad_to(gy_across, 2, lanes), pick, spread
    )
    contract = (((0,), (0,)), ((), ()))
    mixed_cells = lax.all_to_all(mixed, "row", 0, 2, tiled=True).reshape(-1, e_dim)
    out_part = lax.dot_general(
        mixed.reshape(-1, width), grad_all.reshape(-1, c_dim), contract, preferred_element_type=F32
    )
    out_sum = lax.psum_scatter(out_part, "col", scatter_dimension=0, tiled=True)
    out_rows = lax.all_gather(out_sum.astype(BF16), "row", axis=0)
    back_bf, out_rows, mixed_cells, w_perm = lax.optimization_barrier((back_bf, out_rows, mixed_cells, w_perm))
    grad_out_w = lax.all_to_all(out_rows, "col", 0, 1, tiled=True).reshape(e_dim // nc, c_dim)
    dact_down, dproj_down = run_backward(
        act_down, proj_down, params_down, start_down, pad_to(back_bf, 2, lanes), pick, spread
    )
    dproj_down, grad_out_w = lax.optimization_barrier((dproj_down, grad_out_w))
    unpair = lambda values: jnp.concatenate([values[0], values[1]], axis=-1)
    returned = lax.all_to_all(
        swap(jnp.concatenate([dact_across[..., :width], unpair(dproj_across)], axis=-1).astype(BF16)),
        "col", 1, 0, tiled=True,
    )
    dproj = jnp.concatenate([unpair(dproj_down), returned[..., width:].astype(F32)], axis=-1)
    dproj = lax.all_to_all(
        dproj.astype(BF16).reshape(nr, rows, cols, dirs * coefs), "row", 0, 0, tiled=True
    )
    dproj = jnp.sum(dproj.astype(F32), axis=0)
    dproj = lax.all_gather(dproj.astype(BF16), "row", axis=0, tiled=True)
    proj_rows = lax.dynamic_slice_in_dim(proj_weight, me * width, width, axis=0)
    back_active = lax.dot_general(
        dproj.reshape(-1, dirs * coefs), proj_rows, (((1,), (1,)), ((), ())), preferred_element_type=F32
    ).reshape(all_rows, cols, width)
    back_active = back_active + dact_down[..., :width] + returned[..., :width].astype(F32)
    conv_sig = jax.nn.sigmoid(convolved)
    back_conv = back_active * (conv_sig * (1.0 + convolved * (1.0 - conv_sig)))
    grad_padded = col_halo(back_conv)
    back_source = jnp.zeros(source.shape, F32)
    for a in range(3):
        for b in range(3):
            back_source = back_source + grad_padded[2 - a : 2 - a + all_rows, 2 - b : 2 - b + cols] * taps[a, b]
    back_xz = jnp.concatenate([back_source.astype(BF16), back_gate.astype(BF16)], axis=-1)

    result = field.astype(F32) + jnp.dot(mixed_cells, out_full, preferred_element_type=F32).reshape(field.shape)
    xz_cells = lax.all_to_all(back_xz, "row", 0, 2, tiled=True).reshape(-1, 2 * e_dim)
    grad_field = grad_out.astype(F32) + lax.dot_general(
        xz_cells, w_perm, (((1,), (1,)), ((), ())), preferred_element_type=F32
    ).reshape(field.shape)
    in_part = lax.dot_general(
        field_flat, back_xz.reshape(-1, 2 * width), contract, preferred_element_type=F32
    )
    in_sum = lax.psum(in_part, "col")
    g_src, g_gate = in_sum[:, :width], in_sum[:, width:]
    back_one = lax.ppermute(jnp.where(even, g_src, g_gate), "row", reverse_moves(moves_one))
    back_two = lax.ppermute(jnp.where(even, g_gate, g_src), "row", reverse_moves(moves_two))
    grad_in = jnp.concatenate(
        [jnp.where(low, back_one, back_two), jnp.where(low, back_two, back_one)], axis=1
    )
    return (result.astype(BF16), grad_field, grad_in, grad_out_w.astype(F32))


def solution(mesh):
    in_specs = (
        P("row", "col", None), P(None, "row"), P(), P(), P(), P(), P(), P(), P(), P("col", None), P("row", "col", None),
    )
    out_specs = (P("row", "col", None), P("row", "col", None), P(None, "row"), P("col", None))
    return jax.shard_map(local, mesh=mesh, in_specs=in_specs, out_specs=out_specs, check_vma=False)
```

```python
import math

import jax
import jax.numpy as jnp
from jax import lax
from jax.experimental import pallas as pl
from jax.experimental.pallas import tpu as pltpu
from jax.sharding import PartitionSpec as P

DT_FLOOR = 0.004
NORM_EPS = 1e-05
LOG2E = math.log2(math.e)
LN2 = math.log(2.0)
LANES = 128
F32 = jnp.float32
BF16 = jnp.bfloat16


def softplus(v):
    return jnp.maximum(v, 0.0) + jnp.log1p(jnp.exp(-jnp.abs(v)))


def fill_steps(proj_ref, dtw_ref, bias_ref, raw_ref, step_ref):
    length, lines, width = proj_ref.shape
    chunk = 16

    @pl.loop(0, length // chunk)
    def _(c):
        rows = proj_ref[pl.ds(c * chunk, chunk)].reshape(chunk * lines, width)
        raw = jnp.dot(rows, dtw_ref[...], preferred_element_type=F32) + bias_ref[0:1, :]
        raw = raw.reshape(chunk, lines, raw.shape[-1])
        if raw_ref is not None:
            raw_ref[pl.ds(c * chunk, chunk)] = raw
        step_ref[pl.ds(c * chunk, chunk)] = DT_FLOOR + softplus(raw)


def spread_coefs(proj_ref, spread_ref, wide_ref):
    length, lines, coefs = proj_ref.shape
    chunk = 16

    @pl.loop(0, length // chunk)
    def _(c):
        at = pl.ds(c * chunk, chunk)
        rows = proj_ref[at].reshape(chunk * lines, coefs)
        for n in range(wide_ref.shape[-1] // 512):
            cut = pl.ds(n * 512, 512)
            out = jnp.dot(rows, spread_ref[:, cut], preferred_element_type=F32)
            wide_ref[at, :, cut] = out.reshape(chunk, lines, 512)


def loop(count, body, carry, unroll):
    def several(i, carry):
        for j in range(unroll):
            carry = body(i * unroll + j, carry)
        return carry

    return lax.fori_loop(0, count // unroll, several, carry)


def forward_kernel(
    states, act_ref, proj_ref, dtw_ref, bias_ref, rate_ref, skip_ref, spread_ref, y_ref, start_ref, step_ref, wide_ref,
):
    k = pl.program_id(0)
    length, lines, width = act_ref.shape
    fill_steps(proj_ref, dtw_ref, bias_ref, None, step_ref)
    spread_coefs(proj_ref, spread_ref, wide_ref)
    zero = jnp.zeros((lines, width), F32)

    def place(i):
        return jnp.where(k == 0, i, length - 1 - i)

    def coef(p, n):
        return wide_ref[p, :, pl.ds(n * width, width)]

    def first(i, carry):
        state, total = carry
        p = place(i)
        step = step_ref[p]
        drive = step * act_ref[p].astype(F32)
        state = tuple(
            jnp.exp2(step * rate_ref[n]) * state[n] + drive * coef(p, n) for n in range(states)
        )
        return state, total + step

    state, total = loop(length, first, ((zero,) * states, zero), 2)
    closed = []
    for n in range(states):
        one = state[n] / (1.0 - jnp.exp2(total * rate_ref[n]))
        start_ref[n] = one
        closed.append(one)

    @pl.when(k == 0)
    def _():
        y_ref[...] = jnp.zeros_like(y_ref)

    skip = jnp.broadcast_to(skip_ref[0:1, :], (lines, width))

    def second(i, state):
        p = place(i)
        step = step_ref[p]
        act = act_ref[p].astype(F32)
        drive = step * act
        y = y_ref[p] + skip * act
        new = []
        for n in range(states):
            one = jnp.exp2(step * rate_ref[n]) * state[n] + drive * coef(p, n)
            y = y + one * coef(p, states + n)
            new.append(one)
        y_ref[p] = y
        return tuple(new)

    loop(length, second, tuple(closed), 2)


def backward_kernel(
    states, act_ref, proj_ref, dtw_ref, dtwt_ref, bias_ref, rate_ref, skip_ref, start_ref, gy_ref, pick_ref, spread_ref,
    dact_ref, dproj_ref, raw_ref, step_ref, h_ref, wide_ref, prod_ref, draw_ref,
):
    k = pl.program_id(0)
    length, lines, width = act_ref.shape
    fill_steps(proj_ref, dtw_ref, bias_ref, raw_ref, step_ref)
    spread_coefs(proj_ref, spread_ref, wide_ref)
    zero = jnp.zeros((lines, width), F32)

    def place(i):
        return jnp.where(k == 0, i, length - 1 - i)

    def coef(p, n):
        return wide_ref[p, :, pl.ds(n * width, width)]

    for n in range(states):
        h_ref[0, n] = start_ref[n].astype(BF16)

    def replay(i, carry):
        state, total = carry
        p = place(i)
        step = step_ref[p]
        drive = step * act_ref[p].astype(F32)
        new = []
        for n in range(states):
            one = jnp.exp2(step * rate_ref[n]) * state[n] + drive * coef(p, n)
            h_ref[i + 1, n] = one.astype(BF16)
            new.append(one)
        return tuple(new), total + step

    _, total = loop(length, replay, (tuple(start_ref[n] for n in range(states)), zero), 2)

    def adjoint(j, back):
        p = place(length - 1 - j)
        gy = gy_ref[p].astype(F32)
        step = step_ref[p]
        return tuple(
            jnp.exp2(step * rate_ref[n]) * (back[n] + gy * coef(p, states + n)) for n in range(states)
        )

    back = loop(length, adjoint, (zero,) * states, 2)
    back = tuple(back[n] / (1.0 - jnp.exp2(total * rate_ref[n])) for n in range(states))

    @pl.when(k == 0)
    def _():
        dact_ref[...] = jnp.zeros_like(dact_ref)

    skip = jnp.broadcast_to(skip_ref[0:1, :], (lines, width))
    chunk = prod_ref.shape[0]

    def part(c, back):
        first_j = c * chunk

        def last(q, back):
            i = length - 1 - (first_j + q)
            p = place(i)
            gy = gy_ref[p].astype(F32)
            step = step_ref[p]
            act = act_ref[p].astype(F32)
            drive = step * act
            ddrive = zero
            dstep = zero
            new = []
            for n in range(states):
                rate = rate_ref[n]
                lam = back[n] + gy * coef(p, states + n)
                prod_ref[q, :, pl.ds(n * width, width)] = (drive * lam).astype(BF16)
                prod_ref[q, :, pl.ds((states + n) * width, width)] = (gy * h_ref[i + 1, n].astype(F32)).astype(BF16)
                ddrive = ddrive + lam * coef(p, n)
                carried = jnp.exp2(step * rate) * lam
                dstep = dstep + (carried * h_ref[i, n].astype(F32)) * rate
                new.append(carried)
            dstep = LN2 * dstep + act * ddrive
            dact_ref[p] = dact_ref[p] + step * ddrive + skip * gy
            draw_ref[q] = (dstep / (1.0 + jnp.exp(-raw_ref[p]))).astype(BF16)
            return tuple(new)

        back = loop(chunk, last, back, 2)
        prods = prod_ref[...].reshape(chunk * lines, prod_ref.shape[-1])
        raws = draw_ref[...].reshape(chunk * lines, width)
        out = jnp.dot(prods, pick_ref[...], preferred_element_type=F32)
        out = out + jnp.dot(raws, dtwt_ref[...], preferred_element_type=F32)
        out = out.reshape(chunk, lines, out.shape[-1])
        for q in range(chunk):
            dproj_ref[place(length - 1 - (first_j + q))] = out[q]
        return back

    lax.fori_loop(0, length // chunk, part, back)


def whole_spec(shape):
    return pl.BlockSpec(shape, lambda k: (0,) * len(shape))


def each_spec(shape):
    return pl.BlockSpec((None,) + shape, lambda k: (k,) + (0,) * len(shape))


def run_forward(act, proj, params, spread):
    dtw, dtwt, bias, rates, skip, rank, states = params
    length, lines, width = act.shape
    coefs = proj.shape[-1]
    work = 2 * 2 * length * lines * width * states
    return pl.pallas_call(
        lambda *refs: forward_kernel(states, *refs),
        grid=(2,),
        in_specs=[
            whole_spec(act.shape),
            each_spec((length, lines, coefs)),
            each_spec((coefs, width)),
            each_spec((8, width)),
            each_spec((states, lines, width)),
            each_spec((8, width)),
            whole_spec(spread.shape),
        ],
        out_specs=[whole_spec(act.shape), each_spec((states, lines, width))],
        out_shape=[
            jax.ShapeDtypeStruct(act.shape, F32),
            jax.ShapeDtypeStruct((2, states, lines, width), F32),
        ],
        scratch_shapes=[
            pltpu.VMEM(act.shape, F32),
            pltpu.VMEM((length, lines, 2 * states * width), F32),
        ],
        compiler_params=pltpu.CompilerParams(vmem_limit_bytes=56 * 2**20),
        cost_estimate=pl.CostEstimate(flops=10 * work, bytes_accessed=4 * act.size * 4, transcendentals=work),
        name="scan_forward",
    )(act, proj, dtw, bias, rates, skip, spread)


def run_backward(act, proj, params, start, gy, pick, spread):
    dtw, dtwt, bias, rates, skip, rank, states = params
    length, lines, width = act.shape
    coefs = proj.shape[-1]
    work = 2 * 3 * length * lines * width * states
    return pl.pallas_call(
        lambda *refs: backward_kernel(states, *refs),
        grid=(2,),
        in_specs=[
            whole_spec(act.shape),
            each_spec((length, lines, coefs)),
            each_spec((coefs, width)),
            each_spec((width, coefs)),
            each_spec((8, width)),
            each_spec((states, lines, width)),
            each_spec((8, width)),
            each_spec((states, lines, width)),
            whole_spec(act.shape),
            whole_spec(pick.shape),
            whole_spec(spread.shape),
        ],
        out_specs=[whole_spec(act.shape), each_spec((length, lines, coefs))],
        out_shape=[
            jax.ShapeDtypeStruct(act.shape, F32),
            jax.ShapeDtypeStruct((2, length, lines, coefs), F32),
        ],
        scratch_shapes=[
            pltpu.VMEM(act.shape, F32),
            pltpu.VMEM(act.shape, F32),
            pltpu.VMEM((length + 1, states, lines, width), BF16),
            pltpu.VMEM((length, lines, 2 * states * width), F32),
            pltpu.VMEM((8, lines, 2 * states * width), BF16),
            pltpu.VMEM((8, lines, width), BF16),
        ],
        compiler_params=pltpu.CompilerParams(vmem_limit_bytes=60 * 2**20),
        cost_estimate=pl.CostEstimate(flops=10 * work, bytes_accessed=8 * act.size * 4, transcendentals=work),
        name="scan_backward",
    )(act, proj, dtw, dtwt, bias, rates, skip, start, gy, pick, spread)


def pad_to(values, axis, size, fill=0.0):
    missing = size - values.shape[axis]
    if missing == 0:
        return values
    pads = [(0, 0)] * values.ndim
    pads[axis] = (0, missing)
    return jnp.pad(values, pads, constant_values=fill)


def swap(values):
    return jnp.swapaxes(values, 0, 1)


def exchange_kernel(plan, sizes, *refs):
    count = len(plan)
    ins, outs = refs[:count], refs[count : 2 * count]
    send, recv, own = refs[2 * count :]
    axes = sorted({axis for _, axis in plan})
    mesh_ids = pl.DeviceIdType.MESH
    place = {axis: lax.axis_index(axis) for axis in axes}
    barrier = pltpu.get_barrier_semaphore()
    greeted = 0
    for axis in axes:
        for off in range(1, sizes[axis]):
            peer = lax.rem(place[axis] + off, sizes[axis])
            pl.semaphore_signal(barrier, inc=1, device_id={axis: peer}, device_id_type=mesh_ids)
            greeted += 1
    pl.semaphore_wait(barrier, greeted)

    copies, locals_, guarded = [], [], []
    for i, (kind, axis) in enumerate(plan):
        me, peers = place[axis], sizes[axis]
        half = peers // 2

        def remote(src, dst, sent, got, peer, i=i, axis=axis):
            return pltpu.make_async_remote_copy(
                src_ref=src, dst_ref=dst, send_sem=send.at[i, sent], recv_sem=recv.at[i, got],
                device_id={axis: peer}, device_id_type=mesh_ids,
            )

        if kind in ("spread", "gather"):
            for off in range(1, peers):
                peer = lax.rem(me + off, peers)
                src = ins[i].at[peer] if kind == "spread" else ins[i]
                copies.append(remote(src, outs[i].at[me], off, off, peer))
            src = ins[i].at[me] if kind == "spread" else ins[i]
            locals_.append(pltpu.make_async_copy(src, outs[i].at[me], own.at[i]))
        elif kind == "halo":
            copies.append(remote(ins[i].at[1], outs[i].at[0], 0, 0, lax.rem(me + 1, peers)))
            copies.append(remote(ins[i].at[0], outs[i].at[1], 1, 1, lax.rem(me + peers - 1, peers)))
        else:
            for b in range(2):
                if kind == "deal":
                    to, slot, origin = lax.rem(2 * me + b, peers), me // half, b * half + me // 2
                else:
                    to, slot, origin = b * half + me // 2, lax.rem(me, 2), lax.rem(2 * me + b, peers)
                out = remote(ins[i].at[b], outs[i].at[slot], b, slot, to)
                here = pltpu.make_async_copy(ins[i].at[b], outs[i].at[slot], own.at[i])
                arrive = remote(ins[i].at[b], outs[i].at[b], b, b, to)
                guarded.append((to, me, out, here, origin, arrive))
    for copy in copies:
        copy.start()
    for to, me, out, here, _, _ in guarded:
        pl.when(to != me)(out.start)
        pl.when(to == me)(here.start)
    for copy in locals_:
        copy.start()
    for copy in copies:
        copy.wait()
    for to, me, out, here, origin, arrive in guarded:
        pl.when(to != me)(out.wait_send)
        pl.when(to == me)(here.wait)
        pl.when(origin != me)(arrive.wait_recv)
    for copy in locals_:
        copy.wait()


def exchange(stage, *items):
    plan = tuple((kind, axis) for kind, axis, _ in items)
    arrays = [values for _, _, values in items]
    sizes = {axis: lax.axis_size(axis) for _, axis in plan}
    shapes = [
        jax.ShapeDtypeStruct(
            (sizes[axis],) + values.shape if kind == "gather" else values.shape, values.dtype
        )
        for kind, axis, values in items
    ]
    most = max(max(sizes.values()), 2)
    anywhere = pl.BlockSpec(memory_space=pl.ANY)
    return pl.pallas_call(
        lambda *refs: exchange_kernel(plan, sizes, *refs),
        in_specs=[anywhere] * len(items),
        out_specs=[anywhere] * len(items),
        out_shape=shapes,
        scratch_shapes=[
            pltpu.SemaphoreType.DMA((len(items), most)),
            pltpu.SemaphoreType.DMA((len(items), most)),
            pltpu.SemaphoreType.DMA((len(items),)),
        ],
        compiler_params=pltpu.CompilerParams(collective_id=stage, has_side_effects=True),
        name="exchange_%d" % stage,
    )(*arrays)


def parts(values, axis, count):
    shape = values.shape
    cut = values.reshape(shape[:axis] + (count, shape[axis] // count) + shape[axis + 1 :])
    return jnp.moveaxis(cut, axis, 0)


def joined(values, axis):
    moved = jnp.moveaxis(values, 0, axis)
    shape = moved.shape
    return moved.reshape(shape[:axis] + (shape[axis] * shape[axis + 1],) + shape[axis + 2 :])


def edges(cells):
    return jnp.stack([cells[:, 0], cells[:, -1]])


def with_edges(cells, got):
    wide = jnp.concatenate([got[0][:, None], cells, got[1][:, None]], axis=1)
    return jnp.concatenate([wide[-1:], wide, wide[:1]], axis=0)


def local(
    field, in_weight, conv_weight, proj_weight, dt_weight, dt_bias, decay_rate, skip_gain, norm_gain, out_weight, grad_out,
):
    rows, cols, c_dim = field.shape
    dirs, rank, e_dim = dt_weight.shape
    states = decay_rate.shape[1]
    coefs = rank + 2 * states
    nr, nc = lax.axis_size("row"), lax.axis_size("col")
    me = lax.axis_index("row")
    all_rows, width = rows * nr, e_dim // nr

    def mine(values):
        return lax.dynamic_slice_in_dim(values, me * width, width, axis=values.ndim - 1)

    dealt, field_all = exchange(
        0, ("deal", "row", parts(in_weight, 1, 2)), ("gather", "row", field)
    )
    field_all = field_all.reshape(all_rows, cols, c_dim)
    w_mine = jnp.concatenate([dealt[0], dealt[1]], axis=1)
    field_flat = field_all.reshape(-1, c_dim)
    xz = jnp.dot(field_flat, w_mine, preferred_element_type=F32).astype(BF16).reshape(all_rows, cols, 2 * width)
    source, gate = xz[..., :width], xz[..., width:].astype(F32)
    grad_all = lax.all_gather(grad_out, "row", axis=0, tiled=True)
    out_full = lax.all_gather(out_weight, "col", axis=0, tiled=True)
    w_perm = lax.all_gather(w_mine, "row", axis=1, tiled=True)

    taps = mine(conv_weight)
    (source_edges,) = exchange(1, ("halo", "col", edges(source)))
    padded = with_edges(source, source_edges)
    convolved = jnp.zeros(source.shape, F32)
    for a in range(3):
        for b in range(3):
            convolved = convolved + padded[a : a + all_rows, b : b + cols].astype(F32) * taps[a, b]
    active = jax.nn.silu(convolved).astype(BF16)

    act_row, act_col = exchange(
        2, ("spread", "row", parts(active, 0, nr)), ("spread", "col", parts(active, 0, nc))
    )
    act_cells = joined(act_row, 2)
    proj_cells = jnp.dot(act_cells.reshape(-1, e_dim), proj_weight, preferred_element_type=F32)
    split = 2 * coefs
    (proj,) = exchange(3, ("gather", "row", proj_cells.astype(BF16).reshape(rows, cols, 2 * split)))
    proj = proj.reshape(all_rows, cols, 2 * split)
    (proj_col,) = exchange(4, ("spread", "col", parts(proj[..., split:], 0, nc)))
    act_down = active
    act_across, across = swap(joined(act_col, 1)), swap(joined(proj_col, 1))
    pair = lambda values: jnp.stack([values[..., :coefs], values[..., coefs:]], axis=0)
    proj_down, proj_across = pair(proj[..., :split]), pair(across)

    lanes = -(-width // LANES) * LANES
    lines = cols
    dtw = pad_to(pad_to(mine(dt_weight), 2, lanes), 1, coefs)
    dtwt = jnp.swapaxes(dtw, 1, 2)
    bias = jnp.broadcast_to(pad_to(mine(dt_bias), 1, lanes)[:, None, :], (dirs, 8, lanes))
    rates = -LOG2E * pad_to(mine(decay_rate), 2, lanes, 1.0)
    skip = jnp.broadcast_to(pad_to(mine(skip_gain), 1, lanes)[:, None, :], (dirs, 8, lanes))

    def params(at, count):
        wide = jnp.broadcast_to(rates[at : at + 2][:, :, None, :], (2, states, count, lanes))
        cut = slice(at, at + 2)
        return dtw[cut], dtwt[cut], bias[cut], wide, skip[cut], rank, states

    params_down, params_across = params(0, act_down.shape[1]), params(2, act_across.shape[1])
    act_down, act_across = pad_to(act_down, 2, lanes), pad_to(act_across, 2, lanes)
    spots = jnp.repeat(jnp.arange(2 * states) + rank, lanes)
    pick = (spots[:, None] == jnp.arange(coefs)[None, :]).astype(BF16)
    spread = pick.T
    y_across, start_across = run_forward(act_across, proj_across, params_across, spread)
    y_down, start_down = run_forward(act_down, proj_down, params_down, spread)
    (y_back,) = exchange(5, ("spread", "col", parts(swap(y_across[..., :width].astype(BF16)), 1, nc)))
    summed = y_down[..., :width] + joined(y_back, 0).astype(F32)

    back_mixed = lax.dot_general(
        grad_all.reshape(-1, c_dim),
        lax.dynamic_slice_in_dim(out_full, me * width, width, axis=0),
        (((1,), (1,)), ((), ())),
        preferred_element_type=F32,
    ).reshape(all_rows, cols, width)
    gain = mine(norm_gain)
    sig = jax.nn.sigmoid(gate)
    silu = gate * sig
    back_norm = back_mixed * silu * gain
    own_mean = jnp.mean(summed, axis=-1)
    shifted = summed - own_mean[..., None]
    stats = jnp.stack(
        [own_mean, jnp.sum(shifted * shifted, -1), jnp.sum(back_norm, -1), jnp.sum(back_norm * shifted, -1)]
    )
    (stats,) = exchange(6, ("gather", "row", stats.reshape(-1, LANES)))
    stats = stats.reshape(nr, 4, all_rows, cols)
    means = stats[:, 0]
    centre = jnp.mean(means, axis=0)
    off = means - centre
    variance = (jnp.sum(stats[:, 1], 0) + width * jnp.sum(off * off, 0)) / e_dim
    scale = lax.rsqrt(variance + NORM_EPS)
    flat_mean = jnp.sum(stats[:, 2], 0) / e_dim
    tilt_mean = scale * jnp.sum(stats[:, 3] + off * stats[:, 2], 0) / e_dim
    hat = (summed - centre[..., None]) * scale[..., None]
    normed = hat * gain
    mixed = (normed * silu).astype(BF16)
    back_gate = back_mixed * normed * (sig * (1.0 + gate * (1.0 - sig)))
    back_summed = scale[..., None] * (back_norm - flat_mean[..., None] - hat * tilt_mean[..., None])
    back_bf = back_summed.astype(BF16)
    contract = (((0,), (0,)), ((), ()))
    out_part = lax.dot_general(
        mixed.reshape(-1, width), grad_all.reshape(-1, c_dim), contract, preferred_element_type=F32
    )
    gy_across, mixed_cells, out_parts = exchange(
        7,
        ("spread", "col", parts(back_bf, 0, nc)),
        ("spread", "row", parts(mixed, 0, nr)),
        ("spread", "col", parts(out_part.astype(BF16), 0, nc)),
    )
    gy_across = swap(joined(gy_across, 1))
    mixed_cells = joined(mixed_cells, 2).reshape(-1, e_dim)
    out_sum = jnp.sum(out_parts.astype(F32), axis=0).astype(BF16)

    dact_across, dproj_across = run_backward(
        act_across, proj_across, params_across, start_across, pad_to(gy_across, 2, lanes), pick, spread
    )
    unpair = lambda values: jnp.concatenate([values[0], values[1]], axis=-1)
    returned = swap(jnp.concatenate([dact_across[..., :width], unpair(dproj_across)], axis=-1).astype(BF16))
    returned, out_rows = exchange(
        8, ("spread", "col", parts(returned, 1, nc)), ("gather", "row", out_sum)
    )
    returned = joined(returned, 0)
    back_bf, w_perm, dact_across = lax.optimization_barrier((back_bf, w_perm, dact_across))
    dact_down, dproj_down = run_backward(
        act_down, proj_down, params_down, start_down, pad_to(back_bf, 2, lanes), pick, spread
    )
    dproj = jnp.concatenate([unpair(dproj_down), returned[..., width:].astype(F32)], axis=-1)
    dproj, out_own = exchange(
        9, ("spread", "row", parts(dproj.astype(BF16), 0, nr)), ("spread", "col", parts(out_rows, 0, nc))
    )
    grad_out_w = jnp.swapaxes(out_own, 0, 1).reshape(e_dim // nc, c_dim)
    dproj = jnp.sum(dproj.astype(F32), axis=0).astype(BF16)
    (dproj,) = exchange(10, ("gather", "row", dproj))
    proj_rows = lax.dynamic_slice_in_dim(proj_weight, me * width, width, axis=0)
    back_active = lax.dot_general(
        dproj.reshape(-1, dirs * coefs), proj_rows, (((1,), (1,)), ((), ())), preferred_element_type=F32
    ).reshape(all_rows, cols, width)
    back_active = back_active + dact_down[..., :width] + returned[..., :width].astype(F32)
    conv_sig = jax.nn.sigmoid(convolved)
    back_conv = back_active * (conv_sig * (1.0 + convolved * (1.0 - conv_sig)))
    (conv_edges,) = exchange(11, ("halo", "col", edges(back_conv)))
    grad_padded = with_edges(back_conv, conv_edges)
    back_source = jnp.zeros(source.shape, F32)
    for a in range(3):
        for b in range(3):
            back_source = back_source + grad_padded[2 - a : 2 - a + all_rows, 2 - b : 2 - b + cols] * taps[a, b]
    back_xz = jnp.concatenate([back_source.astype(BF16), back_gate.astype(BF16)], axis=-1)

    result = field.astype(F32) + jnp.dot(mixed_cells, out_full, preferred_element_type=F32).reshape(field.shape)
    in_part = lax.dot_general(
        field_flat, back_xz.reshape(-1, 2 * width), contract, preferred_element_type=F32
    )
    xz_cells, in_parts = exchange(
        12,
        ("spread", "row", parts(back_xz, 0, nr)),
        ("spread", "col", parts(in_part.astype(BF16), 0, nc)),
    )
    xz_cells = joined(xz_cells, 2).reshape(-1, 2 * e_dim)
    in_sum = jnp.sum(in_parts.astype(F32), axis=0)
    (in_piece,) = exchange(13, ("undeal", "row", parts(in_sum, 1, 2)))
    (grad_in,) = exchange(14, ("gather", "col", jnp.concatenate([in_piece[0], in_piece[1]], axis=1)))
    grad_in = grad_in.reshape(c_dim, 2 * width)
    grad_field = grad_out.astype(F32) + lax.dot_general(
        xz_cells, w_perm, (((1,), (1,)), ((), ())), preferred_element_type=F32
    ).reshape(field.shape)
    return (result.astype(BF16), grad_field, grad_in, grad_out_w.astype(F32))


def solution(mesh):
    in_specs = (
        P("row", "col", None), P(None, "row"), P(), P(), P(), P(), P(), P(), P(), P("col", None), P("row", "col", None),
    )
    out_specs = (P("row", "col", None), P("row", "col", None), P(None, "row"), P("col", None))
    return jax.shard_map(local, mesh=mesh, in_specs=in_specs, out_specs=out_specs, check_vma=False)
```

```python
import math

import jax
import jax.numpy as jnp
from jax import lax
from jax.experimental import pallas as pl
from jax.experimental.pallas import tpu as pltpu
from jax.sharding import PartitionSpec as P

DT_FLOOR = 0.004
NORM_EPS = 1e-05
LOG2E = math.log2(math.e)
LN2 = math.log(2.0)
LANES = 128
F32 = jnp.float32
BF16 = jnp.bfloat16


def softplus(v):
    return jnp.maximum(v, 0.0) + jnp.log1p(jnp.exp(-jnp.abs(v)))


def fill_steps(proj_ref, dtw_ref, bias_ref, raw_ref, step_ref):
    length, lines, width = proj_ref.shape
    chunk = 16

    @pl.loop(0, length // chunk)
    def _(c):
        rows = proj_ref[pl.ds(c * chunk, chunk)].reshape(chunk * lines, width)
        raw = jnp.dot(rows, dtw_ref[...], preferred_element_type=F32) + bias_ref[0:1, :]
        raw = raw.reshape(chunk, lines, raw.shape[-1])
        if raw_ref is not None:
            raw_ref[pl.ds(c * chunk, chunk)] = raw
        step_ref[pl.ds(c * chunk, chunk)] = DT_FLOOR + softplus(raw)


def spread_coefs(proj_ref, spread_ref, wide_ref):
    length, lines, coefs = proj_ref.shape
    chunk = 16

    @pl.loop(0, length // chunk)
    def _(c):
        at = pl.ds(c * chunk, chunk)
        rows = proj_ref[at].reshape(chunk * lines, coefs)
        for n in range(wide_ref.shape[-1] // 512):
            cut = pl.ds(n * 512, 512)
            out = jnp.dot(rows, spread_ref[:, cut], preferred_element_type=F32)
            wide_ref[at, :, cut] = out.reshape(chunk, lines, 512)


def loop(count, body, carry, unroll):
    def several(i, carry):
        for j in range(unroll):
            carry = body(i * unroll + j, carry)
        return carry

    return lax.fori_loop(0, count // unroll, several, carry)


def forward_kernel(
    states, act_ref, proj_ref, dtw_ref, bias_ref, rate_ref, skip_ref, spread_ref, y_ref, start_ref, step_ref, wide_ref,
    wide_rate, *kept,
):
    k = pl.program_id(0)
    length, lines, width = act_ref.shape
    fill_steps(proj_ref, dtw_ref, bias_ref, None, step_ref)
    spread_coefs(proj_ref, spread_ref, wide_ref)
    for n in range(states):
        wide_rate[n] = jnp.broadcast_to(rate_ref[n : n + 1, :], (lines, width))
    rate_ref = wide_rate
    zero = jnp.zeros((lines, width), F32)

    def make_decay(i, n, step):
        decay = jnp.exp2(step * rate_ref[n])
        if kept:
            kept[0][i, n] = decay
        return decay

    def decay_at(i, n, step):
        return kept[0][i, n] if kept else jnp.exp2(step * rate_ref[n])

    def place(i):
        return jnp.where(k == 0, i, length - 1 - i)

    def coef(p, n):
        return wide_ref[p, :, pl.ds(n * width, width)]

    def first(i, carry):
        state, total = carry
        p = place(i)
        step = step_ref[p]
        drive = step * act_ref[p].astype(F32)
        state = tuple(
            make_decay(i, n, step) * state[n] + drive * coef(p, n) for n in range(states)
        )
        return state, total + step

    state, total = loop(length, first, ((zero,) * states, zero), 2)
    closed = []
    for n in range(states):
        one = state[n] / (1.0 - jnp.exp2(total * rate_ref[n]))
        start_ref[n] = one
        closed.append(one)

    @pl.when(k == 0)
    def _():
        y_ref[...] = jnp.zeros_like(y_ref)

    skip = jnp.broadcast_to(skip_ref[0:1, :], (lines, width))

    def second(i, state):
        p = place(i)
        step = step_ref[p]
        act = act_ref[p].astype(F32)
        drive = step * act
        y = y_ref[p] + skip * act
        new = []
        for n in range(states):
            one = decay_at(i, n, step) * state[n] + drive * coef(p, n)
            y = y + one * coef(p, states + n)
            new.append(one)
        y_ref[p] = y
        return tuple(new)

    loop(length, second, tuple(closed), 2)


def backward_kernel(
    states, act_ref, proj_ref, dtw_ref, dtwt_ref, bias_ref, rate_ref, skip_ref, start_ref, gy_ref, pick_ref, spread_ref,
    dact_ref, dproj_ref, raw_ref, step_ref, h_ref, wide_ref, prod_ref, draw_ref,
    wide_rate, *kept,
):
    k = pl.program_id(0)
    length, lines, width = act_ref.shape
    fill_steps(proj_ref, dtw_ref, bias_ref, raw_ref, step_ref)
    spread_coefs(proj_ref, spread_ref, wide_ref)
    for n in range(states):
        wide_rate[n] = jnp.broadcast_to(rate_ref[n : n + 1, :], (lines, width))
    rate_ref = wide_rate
    zero = jnp.zeros((lines, width), F32)

    def make_decay(i, n, step):
        decay = jnp.exp2(step * rate_ref[n])
        if kept:
            kept[0][i, n] = decay
        return decay

    def decay_at(i, n, step):
        return kept[0][i, n] if kept else jnp.exp2(step * rate_ref[n])

    def place(i):
        return jnp.where(k == 0, i, length - 1 - i)

    def coef(p, n):
        return wide_ref[p, :, pl.ds(n * width, width)]

    for n in range(states):
        h_ref[0, n] = start_ref[n].astype(BF16)

    def replay(i, carry):
        state, total = carry
        p = place(i)
        step = step_ref[p]
        drive = step * act_ref[p].astype(F32)
        new = []
        for n in range(states):
            one = make_decay(i, n, step) * state[n] + drive * coef(p, n)
            h_ref[i + 1, n] = one.astype(BF16)
            new.append(one)
        return tuple(new), total + step

    _, total = loop(length, replay, (tuple(start_ref[n] for n in range(states)), zero), 2)

    def adjoint(j, back):
        i = length - 1 - j
        p = place(i)
        gy = gy_ref[p].astype(F32)
        step = step_ref[p]
        return tuple(
            decay_at(i, n, step) * (back[n] + gy * coef(p, states + n)) for n in range(states)
        )

    back = loop(length, adjoint, (zero,) * states, 2)
    back = tuple(back[n] / (1.0 - jnp.exp2(total * rate_ref[n])) for n in range(states))

    @pl.when(k == 0)
    def _():
        dact_ref[...] = jnp.zeros_like(dact_ref)

    skip = jnp.broadcast_to(skip_ref[0:1, :], (lines, width))
    chunk = prod_ref.shape[0]

    def part(c, back):
        first_j = c * chunk

        def last(q, back):
            i = length - 1 - (first_j + q)
            p = place(i)
            gy = gy_ref[p].astype(F32)
            step = step_ref[p]
            act = act_ref[p].astype(F32)
            drive = step * act
            ddrive = zero
            dstep = zero
            new = []
            for n in range(states):
                rate = rate_ref[n]
                lam = back[n] + gy * coef(p, states + n)
                prod_ref[q, :, pl.ds(n * width, width)] = (drive * lam).astype(BF16)
                prod_ref[q, :, pl.ds((states + n) * width, width)] = (gy * h_ref[i + 1, n].astype(F32)).astype(BF16)
                ddrive = ddrive + lam * coef(p, n)
                carried = decay_at(i, n, step) * lam
                dstep = dstep + (carried * h_ref[i, n].astype(F32)) * rate
                new.append(carried)
            dstep = LN2 * dstep + act * ddrive
            dact_ref[p] = dact_ref[p] + step * ddrive + skip * gy
            draw_ref[q] = (dstep / (1.0 + jnp.exp(-raw_ref[p]))).astype(BF16)
            return tuple(new)

        back = loop(chunk, last, back, 2)
        prods = prod_ref[...].reshape(chunk * lines, prod_ref.shape[-1])
        raws = draw_ref[...].reshape(chunk * lines, width)
        out = jnp.dot(prods, pick_ref[...], preferred_element_type=F32)
        out = out + jnp.dot(raws, dtwt_ref[...], preferred_element_type=F32)
        out = out.reshape(chunk, lines, out.shape[-1])
        for q in range(chunk):
            dproj_ref[place(length - 1 - (first_j + q))] = out[q]
        return back

    lax.fori_loop(0, length // chunk, part, back)


def whole_spec(shape):
    return pl.BlockSpec(shape, lambda k: (0,) * len(shape))


def each_spec(shape, first=0):
    return pl.BlockSpec((None,) + shape, lambda k: (first + k,) + (0,) * len(shape))


def decay_room(length, states, lines, width, taken):
    size = length * states * lines * width
    return [pltpu.VMEM((length, states, lines, width), F32)] if 4 * size + taken <= 48 * 2**20 else []


def run_forward(act, proj, params, spread):
    dtw, dtwt, bias, rates, skip, states, first = params
    length, lines, width = act.shape
    big = length * lines * 2 * states * width
    coefs = proj.shape[-1]
    work = 2 * 2 * length * lines * width * states
    return pl.pallas_call(
        lambda *refs: forward_kernel(states, *refs),
        grid=(2,),
        in_specs=[
            whole_spec(act.shape),
            each_spec((length, lines, coefs)),
            each_spec((coefs, width), first),
            each_spec((8, width), first),
            each_spec((states, width), first),
            each_spec((8, width), first),
            whole_spec(spread.shape),
        ],
        out_specs=[whole_spec(act.shape), each_spec((states, lines, width))],
        out_shape=[
            jax.ShapeDtypeStruct(act.shape, F32),
            jax.ShapeDtypeStruct((2, states, lines, width), F32),
        ],
        scratch_shapes=[
            pltpu.VMEM(act.shape, F32),
            pltpu.VMEM((length, lines, 2 * states * width), F32),
            pltpu.VMEM((states, lines, width), F32),
        ]
        + decay_room(length, states, lines, width, 4 * big),
        compiler_params=pltpu.CompilerParams(vmem_limit_bytes=56 * 2**20),
        cost_estimate=pl.CostEstimate(flops=10 * work, bytes_accessed=4 * act.size * 4, transcendentals=work),
        name="scan_forward",
    )(act, proj, dtw, bias, rates, skip, spread)


def run_backward(act, proj, params, start, gy, pick, spread):
    dtw, dtwt, bias, rates, skip, states, first = params
    length, lines, width = act.shape
    big = length * lines * 2 * states * width
    coefs = proj.shape[-1]
    work = 2 * 3 * length * lines * width * states
    return pl.pallas_call(
        lambda *refs: backward_kernel(states, *refs),
        grid=(2,),
        in_specs=[
            whole_spec(act.shape),
            each_spec((length, lines, coefs)),
            each_spec((coefs, width), first),
            each_spec((width, coefs), first),
            each_spec((8, width), first),
            each_spec((states, width), first),
            each_spec((8, width), first),
            each_spec((states, lines, width)),
            whole_spec(act.shape),
            whole_spec(pick.shape),
            whole_spec(spread.shape),
        ],
        out_specs=[whole_spec(act.shape), each_spec((length, lines, coefs))],
        out_shape=[
            jax.ShapeDtypeStruct(act.shape, F32),
            jax.ShapeDtypeStruct((2, length, lines, coefs), F32),
        ],
        scratch_shapes=[
            pltpu.VMEM(act.shape, F32),
            pltpu.VMEM(act.shape, F32),
            pltpu.VMEM((length + 1, states, lines, width), BF16),
            pltpu.VMEM((length, lines, 2 * states * width), F32),
            pltpu.VMEM((8, lines, 2 * states * width), BF16),
            pltpu.VMEM((8, lines, width), BF16),
            pltpu.VMEM((states, lines, width), F32),
        ]
        + decay_room(length, states, lines, width, 5 * big),
        compiler_params=pltpu.CompilerParams(vmem_limit_bytes=60 * 2**20),
        cost_estimate=pl.CostEstimate(flops=10 * work, bytes_accessed=8 * act.size * 4, transcendentals=work),
        name="scan_backward",
    )(act, proj, dtw, dtwt, bias, rates, skip, start, gy, pick, spread)


def pad_to(values, axis, size, fill=0.0):
    missing = size - values.shape[axis]
    if missing == 0:
        return values
    pads = [(0, 0)] * values.ndim
    pads[axis] = (0, missing)
    return jnp.pad(values, pads, constant_values=fill)


def swap(values):
    return jnp.swapaxes(values, 0, 1)


def exchange_kernel(plan, sizes, *refs):
    count = len(plan)
    ins, outs = refs[:count], refs[count : 2 * count]
    send, recv, own = refs[2 * count :]
    axes = sorted({axis for _, axis in plan})
    mesh_ids = pl.DeviceIdType.MESH
    place = {axis: lax.axis_index(axis) for axis in axes}
    barrier = pltpu.get_barrier_semaphore()
    greeted = 0
    for axis in axes:
        for off in range(1, sizes[axis]):
            peer = lax.rem(place[axis] + off, sizes[axis])
            pl.semaphore_signal(barrier, inc=1, device_id={axis: peer}, device_id_type=mesh_ids)
            greeted += 1
    pl.semaphore_wait(barrier, greeted)

    copies, locals_, guarded = [], [], []
    for i, (kind, axis) in enumerate(plan):
        me, peers = place[axis], sizes[axis]
        half = peers // 2

        def remote(src, dst, sent, got, peer, i=i, axis=axis):
            return pltpu.make_async_remote_copy(
                src_ref=src, dst_ref=dst, send_sem=send.at[i, sent], recv_sem=recv.at[i, got],
                device_id={axis: peer}, device_id_type=mesh_ids,
            )

        if kind in ("spread", "gather"):
            for off in range(1, peers):
                peer = lax.rem(me + off, peers)
                src = ins[i].at[peer] if kind == "spread" else ins[i]
                copies.append(remote(src, outs[i].at[me], off, off, peer))
            src = ins[i].at[me] if kind == "spread" else ins[i]
            locals_.append(pltpu.make_async_copy(src, outs[i].at[me], own.at[i]))
        elif kind == "halo":
            copies.append(remote(ins[i].at[1], outs[i].at[0], 0, 0, lax.rem(me + 1, peers)))
            copies.append(remote(ins[i].at[0], outs[i].at[1], 1, 1, lax.rem(me + peers - 1, peers)))
        else:
            for b in range(2):
                if kind == "deal":
                    to, slot, origin = lax.rem(2 * me + b, peers), me // half, b * half + me // 2
                else:
                    to, slot, origin = b * half + me // 2, lax.rem(me, 2), lax.rem(2 * me + b, peers)
                out = remote(ins[i].at[b], outs[i].at[slot], b, slot, to)
                here = pltpu.make_async_copy(ins[i].at[b], outs[i].at[slot], own.at[i])
                arrive = remote(ins[i].at[b], outs[i].at[b], b, b, to)
                guarded.append((to, me, out, here, origin, arrive))
    for copy in copies:
        copy.start()
    for to, me, out, here, _, _ in guarded:
        pl.when(to != me)(out.start)
        pl.when(to == me)(here.start)
    for copy in locals_:
        copy.start()
    for copy in copies:
        copy.wait()
    for to, me, out, here, origin, arrive in guarded:
        pl.when(to != me)(out.wait_send)
        pl.when(to == me)(here.wait)
        pl.when(origin != me)(arrive.wait_recv)
    for copy in locals_:
        copy.wait()


def exchange(stage, *items):
    plan = tuple((kind, axis) for kind, axis, _ in items)
    arrays = [values for _, _, values in items]
    sizes = {axis: lax.axis_size(axis) for _, axis in plan}
    shapes = [
        jax.ShapeDtypeStruct(
            (sizes[axis],) + values.shape if kind == "gather" else values.shape, values.dtype
        )
        for kind, axis, values in items
    ]
    most = max(max(sizes.values()), 2)
    anywhere = pl.BlockSpec(memory_space=pl.ANY)
    return pl.pallas_call(
        lambda *refs: exchange_kernel(plan, sizes, *refs),
        in_specs=[anywhere] * len(items),
        out_specs=[anywhere] * len(items),
        out_shape=shapes,
        scratch_shapes=[
            pltpu.SemaphoreType.DMA((len(items), most)),
            pltpu.SemaphoreType.DMA((len(items), most)),
            pltpu.SemaphoreType.DMA((len(items),)),
        ],
        compiler_params=pltpu.CompilerParams(collective_id=stage, has_side_effects=True),
        name="exchange_%d" % stage,
    )(*arrays)


def parts(values, axis, count):
    shape = values.shape
    cut = values.reshape(shape[:axis] + (count, shape[axis] // count) + shape[axis + 1 :])
    return jnp.moveaxis(cut, axis, 0)


def joined(values, axis):
    moved = jnp.moveaxis(values, 0, axis)
    shape = moved.shape
    return moved.reshape(shape[:axis] + (shape[axis] * shape[axis + 1],) + shape[axis + 2 :])


def edges(cells):
    return jnp.stack([cells[:, 0], cells[:, -1]])


def with_edges(cells, got):
    wide = jnp.concatenate([got[0][:, None], cells, got[1][:, None]], axis=1)
    return jnp.concatenate([wide[-1:], wide, wide[:1]], axis=0)


def local(
    field, in_weight, conv_weight, proj_weight, dt_weight, dt_bias, decay_rate, skip_gain, norm_gain, out_weight, grad_out,
):
    rows, cols, c_dim = field.shape
    dirs, rank, e_dim = dt_weight.shape
    states = decay_rate.shape[1]
    coefs = rank + 2 * states
    nr, nc = lax.axis_size("row"), lax.axis_size("col")
    me = lax.axis_index("row")
    all_rows, width = rows * nr, e_dim // nr

    def mine(values):
        return lax.dynamic_slice_in_dim(values, me * width, width, axis=values.ndim - 1)

    dealt, field_all = exchange(
        0, ("deal", "row", parts(in_weight, 1, 2)), ("gather", "row", field)
    )
    field_all = field_all.reshape(all_rows, cols, c_dim)
    w_mine = jnp.concatenate([dealt[0], dealt[1]], axis=1)
    field_flat = field_all.reshape(-1, c_dim)
    xz = jnp.dot(field_flat, w_mine, preferred_element_type=F32).astype(BF16).reshape(all_rows, cols, 2 * width)
    source, gate = xz[..., :width], xz[..., width:].astype(F32)
    taps = mine(conv_weight)
    (source_edges,) = exchange(1, ("halo", "col", edges(source)))
    padded = with_edges(source, source_edges)
    convolved = jnp.zeros(source.shape, F32)
    for a in range(3):
        for b in range(3):
            convolved = convolved + padded[a : a + all_rows, b : b + cols].astype(F32) * taps[a, b]
    active = jax.nn.silu(convolved).astype(BF16)

    act_row, act_col = exchange(
        2, ("spread", "row", parts(active, 0, nr)), ("spread", "col", parts(active, 0, nc))
    )
    act_cells = joined(act_row, 2)
    proj_cells = jnp.dot(act_cells.reshape(-1, e_dim), proj_weight, preferred_element_type=F32)
    split = 2 * coefs
    (proj,) = exchange(3, ("gather", "row", proj_cells.astype(BF16).reshape(rows, cols, 2 * split)))
    proj = proj.reshape(all_rows, cols, 2 * split)
    (proj_col,) = exchange(4, ("spread", "col", parts(proj[..., split:], 0, nc)))
    act_down = active
    act_across, across = swap(joined(act_col, 1)), swap(joined(proj_col, 1))
    act_across, later_grad, later_out, later_w = lax.optimization_barrier((act_across, grad_out, out_weight, w_mine))
    grad_all = lax.all_gather(later_grad, "row", axis=0, tiled=True)
    out_full = lax.all_gather(later_out, "col", axis=0, tiled=True)
    w_perm = lax.all_gather(later_w, "row", axis=1, tiled=True)
    pair = lambda values: jnp.stack([values[..., :coefs], values[..., coefs:]], axis=0)
    proj_down, proj_across = pair(proj[..., :split]), pair(across)

    lanes = -(-width // LANES) * LANES
    lines = cols
    dtw = pad_to(pad_to(mine(dt_weight), 2, lanes), 1, coefs)
    dtwt = jnp.swapaxes(dtw, 1, 2)
    bias = jnp.broadcast_to(pad_to(mine(dt_bias), 1, lanes)[:, None, :], (dirs, 8, lanes))
    rates = -LOG2E * pad_to(mine(decay_rate), 2, lanes, 1.0)
    skip = jnp.broadcast_to(pad_to(mine(skip_gain), 1, lanes)[:, None, :], (dirs, 8, lanes))

    params_down = (dtw, dtwt, bias, rates, skip, states, 0)
    params_across = (dtw, dtwt, bias, rates, skip, states, 2)
    act_down, act_across = pad_to(act_down, 2, lanes), pad_to(act_across, 2, lanes)
    spots = jnp.repeat(jnp.arange(2 * states) + rank, lanes)
    pick = (spots[:, None] == jnp.arange(coefs)[None, :]).astype(BF16)
    spread = pick.T
    y_across, start_across = run_forward(act_across, proj_across, params_across, spread)
    y_down, start_down = run_forward(act_down, proj_down, params_down, spread)
    y_back = lax.all_to_all(swap(y_across[..., :width].astype(BF16)), "col", 1, 0, tiled=True)
    summed = y_down[..., :width] + y_back.astype(F32)

    back_mixed = lax.dot_general(
        grad_all.reshape(-1, c_dim),
        lax.dynamic_slice_in_dim(out_full, me * width, width, axis=0),
        (((1,), (1,)), ((), ())),
        preferred_element_type=F32,
    ).reshape(all_rows, cols, width)
    gain = mine(norm_gain)
    sig = jax.nn.sigmoid(gate)
    silu = gate * sig
    back_norm = back_mixed * silu * gain
    own_mean = jnp.mean(summed, axis=-1)
    shifted = summed - own_mean[..., None]
    stats = jnp.stack(
        [own_mean, jnp.sum(shifted * shifted, -1), jnp.sum(back_norm, -1), jnp.sum(back_norm * shifted, -1)]
    )
    (stats,) = exchange(6, ("gather", "row", stats.reshape(-1, LANES)))
    stats = stats.reshape(nr, 4, all_rows, cols)
    means = stats[:, 0]
    centre = jnp.mean(means, axis=0)
    off = means - centre
    variance = (jnp.sum(stats[:, 1], 0) + width * jnp.sum(off * off, 0)) / e_dim
    scale = lax.rsqrt(variance + NORM_EPS)
    flat_mean = jnp.sum(stats[:, 2], 0) / e_dim
    tilt_mean = scale * jnp.sum(stats[:, 3] + off * stats[:, 2], 0) / e_dim
    hat = (summed - centre[..., None]) * scale[..., None]
    normed = hat * gain
    mixed = (normed * silu).astype(BF16)
    back_gate = back_mixed * normed * (sig * (1.0 + gate * (1.0 - sig)))
    back_summed = scale[..., None] * (back_norm - flat_mean[..., None] - hat * tilt_mean[..., None])
    back_bf = back_summed.astype(BF16)
    contract = (((0,), (0,)), ((), ()))
    out_part = lax.dot_general(
        mixed.reshape(-1, width), grad_all.reshape(-1, c_dim), contract, preferred_element_type=F32
    )
    gy_across, mixed_cells, out_parts = exchange(
        7,
        ("spread", "col", parts(back_bf, 0, nc)),
        ("spread", "row", parts(mixed, 0, nr)),
        ("spread", "col", parts(out_part.astype(BF16), 0, nc)),
    )
    gy_across = swap(joined(gy_across, 1))
    mixed_cells = joined(mixed_cells, 2).reshape(-1, e_dim)
    out_sum = jnp.sum(out_parts.astype(F32), axis=0).astype(BF16)

    dact_across, dproj_across = run_backward(
        act_across, proj_across, params_across, start_across, pad_to(gy_across, 2, lanes), pick, spread
    )
    unpair = lambda values: jnp.concatenate([values[0], values[1]], axis=-1)
    returned = swap(jnp.concatenate([dact_across[..., :width], unpair(dproj_across)], axis=-1).astype(BF16))
    returned = lax.all_to_all(returned, "col", 1, 0, tiled=True)
    back_bf, w_perm, dact_across = lax.optimization_barrier((back_bf, w_perm, dact_across))
    dact_down, dproj_down = run_backward(
        act_down, proj_down, params_down, start_down, pad_to(back_bf, 2, lanes), pick, spread
    )
    dproj = jnp.concatenate([unpair(dproj_down), returned[..., width:].astype(F32)], axis=-1)
    dproj, out_rows = exchange(
        9, ("spread", "row", parts(dproj.astype(BF16), 0, nr)), ("gather", "row", out_sum)
    )
    dproj = jnp.sum(dproj.astype(F32), axis=0).astype(BF16)
    dproj, out_own = exchange(10, ("gather", "row", dproj), ("spread", "col", parts(out_rows, 0, nc)))
    grad_out_w = jnp.swapaxes(out_own, 0, 1).reshape(e_dim // nc, c_dim)
    proj_rows = lax.dynamic_slice_in_dim(proj_weight, me * width, width, axis=0)
    back_active = lax.dot_general(
        dproj.reshape(-1, dirs * coefs), proj_rows, (((1,), (1,)), ((), ())), preferred_element_type=F32
    ).reshape(all_rows, cols, width)
    back_active = back_active + dact_down[..., :width] + returned[..., :width].astype(F32)
    conv_sig = jax.nn.sigmoid(convolved)
    back_conv = back_active * (conv_sig * (1.0 + convolved * (1.0 - conv_sig)))
    (conv_edges,) = exchange(11, ("halo", "col", edges(back_conv)))
    grad_padded = with_edges(back_conv, conv_edges)
    back_source = jnp.zeros(source.shape, F32)
    for a in range(3):
        for b in range(3):
            back_source = back_source + grad_padded[2 - a : 2 - a + all_rows, 2 - b : 2 - b + cols] * taps[a, b]
    back_xz = jnp.concatenate([back_source.astype(BF16), back_gate.astype(BF16)], axis=-1)

    result = field.astype(F32) + jnp.dot(mixed_cells, out_full, preferred_element_type=F32).reshape(field.shape)
    in_part = lax.dot_general(
        field_flat, back_xz.reshape(-1, 2 * width), contract, preferred_element_type=F32
    )
    xz_cells, in_parts = exchange(
        12,
        ("spread", "row", parts(back_xz, 0, nr)),
        ("spread", "col", parts(in_part.astype(BF16), 0, nc)),
    )
    xz_cells = joined(xz_cells, 2).reshape(-1, 2 * e_dim)
    in_sum = jnp.sum(in_parts.astype(F32), axis=0)
    (in_piece,) = exchange(13, ("undeal", "row", parts(in_sum.astype(BF16), 1, 2)))
    (grad_in,) = exchange(14, ("gather", "col", jnp.concatenate([in_piece[0], in_piece[1]], axis=1)))
    grad_in = grad_in.reshape(c_dim, 2 * width).astype(F32)
    grad_field = grad_out.astype(F32) + lax.dot_general(
        xz_cells, w_perm, (((1,), (1,)), ((), ())), preferred_element_type=F32
    ).reshape(field.shape)
    return (result.astype(BF16), grad_field, grad_in, grad_out_w.astype(F32))


def solution(mesh):
    in_specs = (
        P("row", "col", None), P(None, "row"), P(), P(), P(), P(), P(), P(), P(), P("col", None), P("row", "col", None),
    )
    out_specs = (P("row", "col", None), P("row", "col", None), P(None, "row"), P("col", None))
    return jax.shard_map(local, mesh=mesh, in_specs=in_specs, out_specs=out_specs, check_vma=False)
```

```python
import math

import jax
import jax.numpy as jnp
from jax import lax
from jax.experimental import pallas as pl
from jax.experimental.pallas import tpu as pltpu
from jax.sharding import PartitionSpec as P

DT_FLOOR = 0.004
NORM_EPS = 1e-05
LOG2E = math.log2(math.e)
LN2 = math.log(2.0)
LANES = 128
F32 = jnp.float32
BF16 = jnp.bfloat16


def softplus(v):
    return jnp.maximum(v, 0.0) + jnp.log1p(jnp.exp(-jnp.abs(v)))


def fill_steps(proj_ref, dtw_ref, bias_ref, raw_ref, step_ref):
    length, lines, width = proj_ref.shape
    chunk = 16

    @pl.loop(0, length // chunk)
    def _(c):
        rows = proj_ref[pl.ds(c * chunk, chunk)].reshape(chunk * lines, width)
        raw = jnp.dot(rows, dtw_ref[...], preferred_element_type=F32) + bias_ref[0:1, :]
        raw = raw.reshape(chunk, lines, raw.shape[-1])
        if raw_ref is not None:
            raw_ref[pl.ds(c * chunk, chunk)] = raw
        step_ref[pl.ds(c * chunk, chunk)] = DT_FLOOR + softplus(raw)


def spread_coefs(proj_ref, spread_ref, wide_ref):
    length, lines, coefs = proj_ref.shape
    chunk = 16

    @pl.loop(0, length // chunk)
    def _(c):
        at = pl.ds(c * chunk, chunk)
        rows = proj_ref[at].reshape(chunk * lines, coefs)
        for n in range(wide_ref.shape[-1] // 512):
            cut = pl.ds(n * 512, 512)
            out = jnp.dot(rows, spread_ref[:, cut], preferred_element_type=F32)
            wide_ref[at, :, cut] = out.reshape(chunk, lines, 512)


def loop(count, body, carry, unroll):
    def several(i, carry):
        for j in range(unroll):
            carry = body(i * unroll + j, carry)
        return carry

    return lax.fori_loop(0, count // unroll, several, carry)


def forward_kernel(
    states, act_ref, proj_ref, dtw_ref, bias_ref, rate_ref, skip_ref, spread_ref, y_ref, start_ref, step_ref, wide_ref,
    wide_rate, *kept,
):
    k = pl.program_id(0)
    length, lines, width = act_ref.shape
    fill_steps(proj_ref, dtw_ref, bias_ref, None, step_ref)
    spread_coefs(proj_ref, spread_ref, wide_ref)
    for n in range(states):
        wide_rate[n] = jnp.broadcast_to(rate_ref[n : n + 1, :], (lines, width))
    rate_ref = wide_rate
    zero = jnp.zeros((lines, width), F32)

    def make_decay(i, n, step):
        decay = jnp.exp2(step * rate_ref[n])
        if kept:
            kept[0][i, n] = decay
        return decay

    def decay_at(i, n, step):
        return kept[0][i, n] if kept else jnp.exp2(step * rate_ref[n])

    def place(i):
        return jnp.where(k == 0, i, length - 1 - i)

    def coef(p, n):
        return wide_ref[p, :, pl.ds(n * width, width)]

    def first(i, carry):
        state, total = carry
        p = place(i)
        step = step_ref[p]
        drive = step * act_ref[p].astype(F32)
        state = tuple(
            make_decay(i, n, step) * state[n] + drive * coef(p, n) for n in range(states)
        )
        return state, total + step

    state, total = loop(length, first, ((zero,) * states, zero), 4)
    closed = []
    for n in range(states):
        one = state[n] / (1.0 - jnp.exp2(total * rate_ref[n]))
        start_ref[n] = one
        closed.append(one)

    @pl.when(k == 0)
    def _():
        y_ref[...] = jnp.zeros_like(y_ref)

    skip = jnp.broadcast_to(skip_ref[0:1, :], (lines, width))

    def second(i, state):
        p = place(i)
        step = step_ref[p]
        act = act_ref[p].astype(F32)
        drive = step * act
        y = y_ref[p] + skip * act
        new = []
        for n in range(states):
            one = decay_at(i, n, step) * state[n] + drive * coef(p, n)
            y = y + one * coef(p, states + n)
            new.append(one)
        y_ref[p] = y
        return tuple(new)

    loop(length, second, tuple(closed), 4)


def backward_kernel(
    states, act_ref, proj_ref, dtw_ref, dtwt_ref, bias_ref, rate_ref, skip_ref, start_ref, gy_ref, pick_ref, spread_ref,
    dact_ref, dproj_ref, raw_ref, step_ref, h_ref, wide_ref, prod_ref, draw_ref,
    wide_rate, *kept,
):
    k = pl.program_id(0)
    length, lines, width = act_ref.shape
    fill_steps(proj_ref, dtw_ref, bias_ref, raw_ref, step_ref)
    spread_coefs(proj_ref, spread_ref, wide_ref)
    for n in range(states):
        wide_rate[n] = jnp.broadcast_to(rate_ref[n : n + 1, :], (lines, width))
    rate_ref = wide_rate
    zero = jnp.zeros((lines, width), F32)

    def make_decay(i, n, step):
        decay = jnp.exp2(step * rate_ref[n])
        if kept:
            kept[0][i, n] = decay
        return decay

    def decay_at(i, n, step):
        return kept[0][i, n] if kept else jnp.exp2(step * rate_ref[n])

    def place(i):
        return jnp.where(k == 0, i, length - 1 - i)

    def coef(p, n):
        return wide_ref[p, :, pl.ds(n * width, width)]

    for n in range(states):
        h_ref[0, n] = start_ref[n].astype(BF16)

    def replay(i, carry):
        state, total = carry
        p = place(i)
        step = step_ref[p]
        drive = step * act_ref[p].astype(F32)
        new = []
        for n in range(states):
            one = make_decay(i, n, step) * state[n] + drive * coef(p, n)
            h_ref[i + 1, n] = one.astype(BF16)
            new.append(one)
        return tuple(new), total + step

    _, total = loop(length, replay, (tuple(start_ref[n] for n in range(states)), zero), 4)

    def adjoint(j, back):
        i = length - 1 - j
        p = place(i)
        gy = gy_ref[p].astype(F32)
        step = step_ref[p]
        return tuple(
            decay_at(i, n, step) * (back[n] + gy * coef(p, states + n)) for n in range(states)
        )

    back = loop(length, adjoint, (zero,) * states, 4)
    back = tuple(back[n] / (1.0 - jnp.exp2(total * rate_ref[n])) for n in range(states))

    @pl.when(k == 0)
    def _():
        dact_ref[...] = jnp.zeros_like(dact_ref)

    skip = jnp.broadcast_to(skip_ref[0:1, :], (lines, width))
    chunk = prod_ref.shape[0]

    def part(c, back):
        first_j = c * chunk

        def last(q, back):
            i = length - 1 - (first_j + q)
            p = place(i)
            gy = gy_ref[p].astype(F32)
            step = step_ref[p]
            act = act_ref[p].astype(F32)
            drive = step * act
            ddrive = zero
            dstep = zero
            new = []
            for n in range(states):
                rate = rate_ref[n]
                lam = back[n] + gy * coef(p, states + n)
                prod_ref[q, :, pl.ds(n * width, width)] = (drive * lam).astype(BF16)
                prod_ref[q, :, pl.ds((states + n) * width, width)] = (gy * h_ref[i + 1, n].astype(F32)).astype(BF16)
                ddrive = ddrive + lam * coef(p, n)
                carried = decay_at(i, n, step) * lam
                dstep = dstep + (carried * h_ref[i, n].astype(F32)) * rate
                new.append(carried)
            dstep = LN2 * dstep + act * ddrive
            dact_ref[p] = dact_ref[p] + step * ddrive + skip * gy
            draw_ref[q] = (dstep / (1.0 + jnp.exp(-raw_ref[p]))).astype(BF16)
            return tuple(new)

        back = loop(chunk, last, back, 2)
        prods = prod_ref[...].reshape(chunk * lines, prod_ref.shape[-1])
        raws = draw_ref[...].reshape(chunk * lines, width)
        out = jnp.dot(prods, pick_ref[...], preferred_element_type=F32)
        out = out + jnp.dot(raws, dtwt_ref[...], preferred_element_type=F32)
        out = out.reshape(chunk, lines, out.shape[-1])
        for q in range(chunk):
            dproj_ref[place(length - 1 - (first_j + q))] = out[q]
        return back

    lax.fori_loop(0, length // chunk, part, back)


def whole_spec(shape):
    return pl.BlockSpec(shape, lambda k: (0,) * len(shape))


def each_spec(shape, first=0):
    return pl.BlockSpec((None,) + shape, lambda k: (first + k,) + (0,) * len(shape))


def decay_room(length, states, lines, width, taken):
    size = length * states * lines * width
    return [pltpu.VMEM((length, states, lines, width), F32)] if 4 * size + taken <= 48 * 2**20 else []


def run_forward(act, proj, params, spread):
    dtw, dtwt, bias, rates, skip, states, first = params
    length, lines, width = act.shape
    big = length * lines * 2 * states * width
    coefs = proj.shape[-1]
    work = 2 * 2 * length * lines * width * states
    return pl.pallas_call(
        lambda *refs: forward_kernel(states, *refs),
        grid=(2,),
        in_specs=[
            whole_spec(act.shape),
            each_spec((length, lines, coefs)),
            each_spec((coefs, width), first),
            each_spec((8, width), first),
            each_spec((states, width), first),
            each_spec((8, width), first),
            whole_spec(spread.shape),
        ],
        out_specs=[whole_spec(act.shape), each_spec((states, lines, width))],
        out_shape=[
            jax.ShapeDtypeStruct(act.shape, F32),
            jax.ShapeDtypeStruct((2, states, lines, width), F32),
        ],
        scratch_shapes=[
            pltpu.VMEM(act.shape, F32),
            pltpu.VMEM((length, lines, 2 * states * width), F32),
            pltpu.VMEM((states, lines, width), F32),
        ]
        + decay_room(length, states, lines, width, 4 * big),
        compiler_params=pltpu.CompilerParams(vmem_limit_bytes=56 * 2**20),
        cost_estimate=pl.CostEstimate(flops=10 * work, bytes_accessed=4 * act.size * 4, transcendentals=work),
        name="scan_forward",
    )(act, proj, dtw, bias, rates, skip, spread)


def run_backward(act, proj, params, start, gy, pick, spread):
    dtw, dtwt, bias, rates, skip, states, first = params
    length, lines, width = act.shape
    big = length * lines * 2 * states * width
    coefs = proj.shape[-1]
    work = 2 * 3 * length * lines * width * states
    return pl.pallas_call(
        lambda *refs: backward_kernel(states, *refs),
        grid=(2,),
        in_specs=[
            whole_spec(act.shape),
            each_spec((length, lines, coefs)),
            each_spec((coefs, width), first),
            each_spec((width, coefs), first),
            each_spec((8, width), first),
            each_spec((states, width), first),
            each_spec((8, width), first),
            each_spec((states, lines, width)),
            whole_spec(act.shape),
            whole_spec(pick.shape),
            whole_spec(spread.shape),
        ],
        out_specs=[whole_spec(act.shape), each_spec((length, lines, coefs))],
        out_shape=[
            jax.ShapeDtypeStruct(act.shape, F32),
            jax.ShapeDtypeStruct((2, length, lines, coefs), F32),
        ],
        scratch_shapes=[
            pltpu.VMEM(act.shape, F32),
            pltpu.VMEM(act.shape, F32),
            pltpu.VMEM((length + 1, states, lines, width), BF16),
            pltpu.VMEM((length, lines, 2 * states * width), F32),
            pltpu.VMEM((8, lines, 2 * states * width), BF16),
            pltpu.VMEM((8, lines, width), BF16),
            pltpu.VMEM((states, lines, width), F32),
        ]
        + decay_room(length, states, lines, width, 5 * big),
        compiler_params=pltpu.CompilerParams(vmem_limit_bytes=60 * 2**20),
        cost_estimate=pl.CostEstimate(flops=10 * work, bytes_accessed=8 * act.size * 4, transcendentals=work),
        name="scan_backward",
    )(act, proj, dtw, dtwt, bias, rates, skip, start, gy, pick, spread)


def pad_to(values, axis, size, fill=0.0):
    missing = size - values.shape[axis]
    if missing == 0:
        return values
    pads = [(0, 0)] * values.ndim
    pads[axis] = (0, missing)
    return jnp.pad(values, pads, constant_values=fill)


def swap(values):
    return jnp.swapaxes(values, 0, 1)


def exchange_kernel(plan, sizes, *refs):
    count = len(plan)
    ins, outs = refs[:count], refs[count : 2 * count]
    send, recv, own = refs[2 * count :]
    axes = sorted({axis for _, axis in plan})
    mesh_ids = pl.DeviceIdType.MESH
    place = {axis: lax.axis_index(axis) for axis in axes}
    barrier = pltpu.get_barrier_semaphore()
    greeted = 0
    for axis in axes:
        for off in range(1, sizes[axis]):
            peer = lax.rem(place[axis] + off, sizes[axis])
            pl.semaphore_signal(barrier, inc=1, device_id={axis: peer}, device_id_type=mesh_ids)
            greeted += 1
    pl.semaphore_wait(barrier, greeted)

    copies, locals_, guarded = [], [], []
    for i, (kind, axis) in enumerate(plan):
        me, peers = place[axis], sizes[axis]
        half = peers // 2

        def remote(src, dst, sent, got, peer, i=i, axis=axis):
            return pltpu.make_async_remote_copy(
                src_ref=src, dst_ref=dst, send_sem=send.at[i, sent], recv_sem=recv.at[i, got],
                device_id={axis: peer}, device_id_type=mesh_ids,
            )

        if kind in ("spread", "gather"):
            for off in range(1, peers):
                peer = lax.rem(me + off, peers)
                src = ins[i].at[peer] if kind == "spread" else ins[i]
                copies.append(remote(src, outs[i].at[me], off, off, peer))
            src = ins[i].at[me] if kind == "spread" else ins[i]
            locals_.append(pltpu.make_async_copy(src, outs[i].at[me], own.at[i]))
        elif kind == "halo":
            copies.append(remote(ins[i].at[1], outs[i].at[0], 0, 0, lax.rem(me + 1, peers)))
            copies.append(remote(ins[i].at[0], outs[i].at[1], 1, 1, lax.rem(me + peers - 1, peers)))
        else:
            for b in range(2):
                if kind == "deal":
                    to, slot, origin = lax.rem(2 * me + b, peers), me // half, b * half + me // 2
                else:
                    to, slot, origin = b * half + me // 2, lax.rem(me, 2), lax.rem(2 * me + b, peers)
                out = remote(ins[i].at[b], outs[i].at[slot], b, slot, to)
                here = pltpu.make_async_copy(ins[i].at[b], outs[i].at[slot], own.at[i])
                arrive = remote(ins[i].at[b], outs[i].at[b], b, b, to)
                guarded.append((to, me, out, here, origin, arrive))
    for copy in copies:
        copy.start()
    for to, me, out, here, _, _ in guarded:
        pl.when(to != me)(out.start)
        pl.when(to == me)(here.start)
    for copy in locals_:
        copy.start()
    for copy in copies:
        copy.wait()
    for to, me, out, here, origin, arrive in guarded:
        pl.when(to != me)(out.wait_send)
        pl.when(to == me)(here.wait)
        pl.when(origin != me)(arrive.wait_recv)
    for copy in locals_:
        copy.wait()


def exchange(stage, *items):
    plan = tuple((kind, axis) for kind, axis, _ in items)
    arrays = [values for _, _, values in items]
    sizes = {axis: lax.axis_size(axis) for _, axis in plan}
    shapes = [
        jax.ShapeDtypeStruct(
            (sizes[axis],) + values.shape if kind == "gather" else values.shape, values.dtype
        )
        for kind, axis, values in items
    ]
    most = max(max(sizes.values()), 2)
    anywhere = pl.BlockSpec(memory_space=pl.ANY)
    return pl.pallas_call(
        lambda *refs: exchange_kernel(plan, sizes, *refs),
        in_specs=[anywhere] * len(items),
        out_specs=[anywhere] * len(items),
        out_shape=shapes,
        scratch_shapes=[
            pltpu.SemaphoreType.DMA((len(items), most)),
            pltpu.SemaphoreType.DMA((len(items), most)),
            pltpu.SemaphoreType.DMA((len(items),)),
        ],
        compiler_params=pltpu.CompilerParams(collective_id=stage, has_side_effects=True),
        name="exchange_%d" % stage,
    )(*arrays)


def parts(values, axis, count):
    shape = values.shape
    cut = values.reshape(shape[:axis] + (count, shape[axis] // count) + shape[axis + 1 :])
    return jnp.moveaxis(cut, axis, 0)


def joined(values, axis):
    moved = jnp.moveaxis(values, 0, axis)
    shape = moved.shape
    return moved.reshape(shape[:axis] + (shape[axis] * shape[axis + 1],) + shape[axis + 2 :])


def edges(cells):
    return jnp.stack([cells[:, 0], cells[:, -1]])


def with_edges(cells, got):
    wide = jnp.concatenate([got[0][:, None], cells, got[1][:, None]], axis=1)
    return jnp.concatenate([wide[-1:], wide, wide[:1]], axis=0)


def local(
    field, in_weight, conv_weight, proj_weight, dt_weight, dt_bias, decay_rate, skip_gain, norm_gain, out_weight, grad_out,
):
    rows, cols, c_dim = field.shape
    dirs, rank, e_dim = dt_weight.shape
    states = decay_rate.shape[1]
    coefs = rank + 2 * states
    nr, nc = lax.axis_size("row"), lax.axis_size("col")
    me = lax.axis_index("row")
    all_rows, width = rows * nr, e_dim // nr

    def mine(values):
        return lax.dynamic_slice_in_dim(values, me * width, width, axis=values.ndim - 1)

    dealt, field_all = exchange(
        0, ("deal", "row", parts(in_weight, 1, 2)), ("gather", "row", field)
    )
    field_all = field_all.reshape(all_rows, cols, c_dim)
    w_mine = jnp.concatenate([dealt[0], dealt[1]], axis=1)
    field_flat = field_all.reshape(-1, c_dim)
    xz = jnp.dot(field_flat, w_mine, preferred_element_type=F32).astype(BF16).reshape(all_rows, cols, 2 * width)
    source, gate = xz[..., :width], xz[..., width:].astype(F32)
    taps = mine(conv_weight)
    (source_edges,) = exchange(1, ("halo", "col", edges(source)))
    padded = with_edges(source, source_edges)
    convolved = jnp.zeros(source.shape, F32)
    for a in range(3):
        for b in range(3):
            convolved = convolved + padded[a : a + all_rows, b : b + cols].astype(F32) * taps[a, b]
    active = jax.nn.silu(convolved).astype(BF16)

    (act_row,) = exchange(2, ("spread", "row", parts(active, 0, nr)))
    act_cells = joined(act_row, 2)
    proj_cells = jnp.dot(act_cells.reshape(-1, e_dim), proj_weight, preferred_element_type=F32)
    split = 2 * coefs
    proj, act_col = exchange(
        3,
        ("gather", "row", proj_cells.astype(BF16).reshape(rows, cols, 2 * split)),
        ("spread", "col", parts(active, 0, nc)),
    )
    proj = proj.reshape(all_rows, cols, 2 * split)
    (proj_col,) = exchange(4, ("spread", "col", parts(proj[..., split:], 0, nc)))
    act_down = active
    act_across, across = swap(joined(act_col, 1)), swap(joined(proj_col, 1))
    across, later_grad, later_out, later_w = lax.optimization_barrier((across, grad_out, out_weight, w_mine))
    grad_all = lax.all_gather(later_grad, "row", axis=0, tiled=True)
    out_full = lax.all_gather(later_out, "col", axis=0, tiled=True)
    w_perm = lax.all_gather(later_w, "row", axis=1, tiled=True)
    pair = lambda values: jnp.stack([values[..., :coefs], values[..., coefs:]], axis=0)
    proj_down, proj_across = pair(proj[..., :split]), pair(across)

    lanes = -(-width // LANES) * LANES
    lines = cols
    dtw = pad_to(pad_to(mine(dt_weight), 2, lanes), 1, coefs)
    dtwt = jnp.swapaxes(dtw, 1, 2)
    bias = jnp.broadcast_to(pad_to(mine(dt_bias), 1, lanes)[:, None, :], (dirs, 8, lanes))
    rates = -LOG2E * pad_to(mine(decay_rate), 2, lanes, 1.0)
    skip = jnp.broadcast_to(pad_to(mine(skip_gain), 1, lanes)[:, None, :], (dirs, 8, lanes))

    params_down = (dtw, dtwt, bias, rates, skip, states, 0)
    params_across = (dtw, dtwt, bias, rates, skip, states, 2)
    act_down, act_across = pad_to(act_down, 2, lanes), pad_to(act_across, 2, lanes)
    spots = jnp.repeat(jnp.arange(2 * states) + rank, lanes)
    pick = (spots[:, None] == jnp.arange(coefs)[None, :]).astype(BF16)
    spread = pick.T
    y_across, start_across = run_forward(act_across, proj_across, params_across, spread)
    y_down, start_down = run_forward(act_down, proj_down, params_down, spread)
    y_back = lax.all_to_all(swap(y_across[..., :width].astype(BF16)), "col", 1, 0, tiled=True)
    summed = y_down[..., :width] + y_back.astype(F32)

    back_mixed = lax.dot_general(
        grad_all.reshape(-1, c_dim),
        lax.dynamic_slice_in_dim(out_full, me * width, width, axis=0),
        (((1,), (1,)), ((), ())),
        preferred_element_type=F32,
    ).reshape(all_rows, cols, width)
    gain = mine(norm_gain)
    sig = jax.nn.sigmoid(gate)
    silu = gate * sig
    back_norm = back_mixed * silu * gain
    own_mean = jnp.mean(summed, axis=-1)
    shifted = summed - own_mean[..., None]
    stats = jnp.stack(
        [own_mean, jnp.sum(shifted * shifted, -1), jnp.sum(back_norm, -1), jnp.sum(back_norm * shifted, -1)]
    )
    (stats,) = exchange(6, ("gather", "row", stats.reshape(-1, LANES)))
    stats = stats.reshape(nr, 4, all_rows, cols)
    means = stats[:, 0]
    centre = jnp.mean(means, axis=0)
    off = means - centre
    variance = (jnp.sum(stats[:, 1], 0) + width * jnp.sum(off * off, 0)) / e_dim
    scale = lax.rsqrt(variance + NORM_EPS)
    flat_mean = jnp.sum(stats[:, 2], 0) / e_dim
    tilt_mean = scale * jnp.sum(stats[:, 3] + off * stats[:, 2], 0) / e_dim
    hat = (summed - centre[..., None]) * scale[..., None]
    normed = hat * gain
    mixed = (normed * silu).astype(BF16)
    back_gate = back_mixed * normed * (sig * (1.0 + gate * (1.0 - sig)))
    back_summed = scale[..., None] * (back_norm - flat_mean[..., None] - hat * tilt_mean[..., None])
    back_bf = back_summed.astype(BF16)
    contract = (((0,), (0,)), ((), ()))
    out_part = lax.dot_general(
        mixed.reshape(-1, width), grad_all.reshape(-1, c_dim), contract, preferred_element_type=F32
    )
    gy_across, mixed_cells = exchange(
        7, ("spread", "col", parts(back_bf, 0, nc)), ("spread", "row", parts(mixed, 0, nr))
    )
    gy_across = swap(joined(gy_across, 1))
    mixed_cells = joined(mixed_cells, 2).reshape(-1, e_dim)

    dact_across, dproj_across = run_backward(
        act_across, proj_across, params_across, start_across, pad_to(gy_across, 2, lanes), pick, spread
    )
    unpair = lambda values: jnp.concatenate([values[0], values[1]], axis=-1)
    returned = swap(jnp.concatenate([dact_across[..., :width], unpair(dproj_across)], axis=-1).astype(BF16))
    returned = lax.all_to_all(returned, "col", 1, 0, tiled=True)
    dact_down, dproj_down = run_backward(
        act_down, proj_down, params_down, start_down, pad_to(back_bf, 2, lanes), pick, spread
    )
    dproj = jnp.concatenate([unpair(dproj_down), returned[..., width:].astype(F32)], axis=-1)
    dproj, out_parts = exchange(
        9,
        ("spread", "row", parts(dproj.astype(BF16), 0, nr)),
        ("spread", "col", parts(out_part.astype(BF16), 0, nc)),
    )
    out_sum = jnp.sum(out_parts.astype(F32), axis=0).astype(BF16)
    dproj = jnp.sum(dproj.astype(F32), axis=0).astype(BF16)
    dproj, out_rows = exchange(10, ("gather", "row", dproj), ("gather", "row", out_sum))
    proj_rows = lax.dynamic_slice_in_dim(proj_weight, me * width, width, axis=0)
    back_active = lax.dot_general(
        dproj.reshape(-1, dirs * coefs), proj_rows, (((1,), (1,)), ((), ())), preferred_element_type=F32
    ).reshape(all_rows, cols, width)
    back_active = back_active + dact_down[..., :width] + returned[..., :width].astype(F32)
    conv_sig = jax.nn.sigmoid(convolved)
    back_conv = back_active * (conv_sig * (1.0 + convolved * (1.0 - conv_sig)))
    conv_edges, out_own = exchange(
        11, ("halo", "col", edges(back_conv)), ("spread", "col", parts(out_rows, 0, nc))
    )
    grad_out_w = jnp.swapaxes(out_own, 0, 1).reshape(e_dim // nc, c_dim)
    grad_padded = with_edges(back_conv, conv_edges)
    back_source = jnp.zeros(source.shape, F32)
    for a in range(3):
        for b in range(3):
            back_source = back_source + grad_padded[2 - a : 2 - a + all_rows, 2 - b : 2 - b + cols] * taps[a, b]
    back_xz = jnp.concatenate([back_source.astype(BF16), back_gate.astype(BF16)], axis=-1)

    result = field.astype(F32) + jnp.dot(mixed_cells, out_full, preferred_element_type=F32).reshape(field.shape)
    in_part = lax.dot_general(
        field_flat, back_xz.reshape(-1, 2 * width), contract, preferred_element_type=F32
    )
    xz_cells, in_parts = exchange(
        12,
        ("spread", "row", parts(back_xz, 0, nr)),
        ("spread", "col", parts(in_part.astype(BF16), 0, nc)),
    )
    xz_cells = joined(xz_cells, 2).reshape(-1, 2 * e_dim)
    in_sum = jnp.sum(in_parts.astype(F32), axis=0)
    (in_piece,) = exchange(13, ("undeal", "row", parts(in_sum.astype(BF16), 1, 2)))
    (grad_in,) = exchange(14, ("gather", "col", jnp.concatenate([in_piece[0], in_piece[1]], axis=1)))
    grad_in = grad_in.reshape(c_dim, 2 * width).astype(F32)
    grad_field = grad_out.astype(F32) + lax.dot_general(
        xz_cells, w_perm, (((1,), (1,)), ((), ())), preferred_element_type=F32
    ).reshape(field.shape)
    return (result.astype(BF16), grad_field, grad_in, grad_out_w.astype(F32))


def solution(mesh):
    in_specs = (
        P("row", "col", None), P(None, "row"), P(), P(), P(), P(), P(), P(), P(), P("col", None), P("row", "col", None),
    )
    out_specs = (P("row", "col", None), P("row", "col", None), P(None, "row"), P("col", None))
    return jax.shard_map(local, mesh=mesh, in_specs=in_specs, out_specs=out_specs, check_vma=False)
```
